512 devices in a mesh: basis: 32 (over z_hi, x, core), aux: 16 (over z_lo, y).
Axes of the slice: x: 4, y: 8, z: 8 (z_hi: 4, z_lo: 2; z = z_hi * 2 + z_lo), core: 2. Of those that a mesh axis runs over, the one named last changes fastest.
Arguments:
- half_three: bfloat16 [16384, 64, 256], P('basis', 'aux'), may hold values from -1.25 to 1.25
- block_mask: int32 [128, 16, 2], P('basis', 'aux'), may hold values 0 or 1
- panel_blocks: int32 [16], replicated, may hold values from 0 to 127, as said below
Outputs:
- exchange_panel: float32 [2048, 16384], P('aux', 'basis')
The draws below stay inside these ranges and needn't reach their ends.
Inputs may be any that keep to these rules, and one draw needn't show every extreme that they name: `panel_blocks`: distinct basis block numbers; no two lie in the same run of 4 blocks, so each device along basis holds at most one, and exactly 16 devices hold one.
All inputs are finite; a program needn't handle non-finite values. No bound on the sum of `block_mask` on one device may be relied on, other than what follows from the above.
Results may differ from the reference program's by a relative error of at most 0.0003.
Values may be sent and summed in bfloat16 or wider, within the bound.
A program may use at most 64 MiB of HBM per device.

```python
import jax
import jax.numpy as jnp
from jax import lax

BLK = 128
NBB = 4
AUXW = 4
NOB = 2
NBT = 128
COLS = 16384
AUX = 64
NAB = 16
OCC = 256
NPB = 16
ROWS = 2048
N_BASIS = 32
N_AUX = 16


def draw_panel_blocks(key, part):
    key = jax.random.fold_in(key, 11)
    first, second, third = jax.random.split(key, 3)
    middle = 1 + jax.random.permutation(first, N_BASIS - 2)[:NPB - 2]
    holders = jnp.concatenate([jnp.array([0, N_BASIS - 1], jnp.int32), middle.astype(jnp.int32)])
    within = jax.random.randint(second, (NPB,), 0, NBB).astype(jnp.int32)
    within = within.at[0].set(0).at[1].set(NBB - 1)
    blocks = holders * NBB + within
    order = jax.random.permutation(third, NPB)
    return blocks[order].astype(jnp.int32)


def touch_ends(values, own_key, smallest, top_value):
    longest = values.shape.index(max(values.shape))
    spots = []
    for shift in (0, 1):
        where = [jax.random.randint(jax.random.fold_in(own_key, axis), (), 0, length) for axis, length in enumerate(values.shape)]
        where[longest] = (where[longest] + shift) % values.shape[longest]
        spots.append(tuple(where))
    return values.at[spots[0]].set(smallest).at[spots[1]].set(top_value)


def block_levels(key, dims, pieces, smallest, top_value):
    factor_of, own = 1.0, jax.random.fold_in(key, 6)
    for axis_at, parts in pieces:
        steps = jnp.exp(jax.random.uniform(jax.random.fold_in(own, axis_at), (parts,), jnp.float32, smallest / len(pieces), top_value / len(pieces)))
        factor_of = factor_of * jnp.repeat(steps, dims[axis_at] // parts).reshape([-1 if axis == axis_at else 1 for axis in range(len(dims))])
    return factor_of


def normal_values(own_key, extent, spread, most, cuts=(), dtype=jnp.bfloat16):
    level = block_levels(own_key, extent, cuts, -0.22, 0.18) if cuts else 1.0
    entries = jax.random.normal(own_key, extent, jnp.float32) * spread * level
    return jnp.minimum(jnp.maximum(entries, -most), most).astype(dtype)


def setup_inputs(seed: int = 0) -> dict:
    seeds = jax.random.split(jax.random.key(seed), 4)
    half_three = normal_values(seeds[0], (COLS, AUX, OCC), 0.0884, 1.25, ((0, 32), (1, 16)))
    block_mask = touch_ends((jax.random.randint(seeds[1], (NBT, NAB, NOB), 0, 4) < 3).astype(jnp.int32), jax.random.fold_in(seeds[1], 1), 0, 1)
    panel_blocks = draw_panel_blocks(jax.random.fold_in(seeds[3], 71), 0)
    return {"half_three": half_three, "block_mask": block_mask, "panel_blocks": panel_blocks}


def reference(half_three, block_mask, panel_blocks):
    shaped = half_three.reshape(NBT, BLK, N_AUX, AUXW, NOB, BLK)
    keep = block_mask[:, None, :, None, :, None].astype(jnp.bfloat16)
    kept = (shaped * keep).reshape(NBT, BLK, AUX * OCC)
    panel = jnp.take(kept, panel_blocks.astype(jnp.int32), axis=0).reshape(ROWS, AUX * OCC)

    def column(block):
        return jnp.dot(panel, block.T, preferred_element_type=jnp.float32)

    result = lax.map(column, kept)
    return jnp.transpose(result, (1, 0, 2)).reshape(ROWS, COLS)
```

```python
import functools

import jax
import jax.numpy as jnp
from jax import lax
from jax.experimental import pallas as pl
from jax.experimental.pallas import tpu as pltpu
from jax.sharding import PartitionSpec as P

MESH = pl.DeviceIdType.MESH
NZH, NX, NCORE, NZL, NY = 4, 4, 2, 2, 8
NPB = 16
BLK = 128
K8 = 8
CHUNKS = 4
LANES = 4
TOP = 32767.0
LEVELS = 64.0
STAGE_AT = {"across": 0, "compact": 6, "share": 11, "multiply": 13, "hop1": 17, "hop2": 21, "hop3": 25, "merge": 29, "finish": 33}
SPACING = 20.0 / CHUNKS


def rank(zh, x, c):
    return (zh * NX + x) * NCORE + c


def wait_bytes(view, sem):
    pltpu.make_async_copy(view, view, sem).wait()


def encode(values, rows, scales, message):
    for i, value in enumerate(values):
        scales[pl.ds(i, 1), :] = jnp.max(jnp.abs(value), axis=0, keepdims=True)
    most = jnp.maximum(scales[...], 1e-33)
    level = jnp.floor(jnp.log(most) * (LEVELS / 0.6931471805599453)) + 2.0
    factor = jnp.exp(level * (-0.6931471805599453 / LEVELS)) * TOP
    for i, value in enumerate(values):
        message[pl.ds(i * rows, rows), :] = jnp.round(value * factor[i : i + 1, :]).astype(jnp.int32).astype(jnp.int16)
    both = jnp.concatenate([level, jnp.zeros_like(level)], axis=0)
    message[pl.ds(8 * rows, 16), :] = both.astype(jnp.int32).astype(jnp.int16)


def decode(message, rows, count):
    level = message[pl.ds(8 * rows, 16), :].astype(jnp.int32).astype(jnp.float32)
    factor = jnp.exp(level * (0.6931471805599453 / LEVELS)) * (1.0 / TOP)
    return [
        message[pl.ds(i * rows, rows), :].astype(jnp.int32).astype(jnp.float32) * factor[i : i + 1, :]
        for i in range(count)
    ]


def kernel(
    kept, slot, holders, out, panel, part, sent, got, fsent, fgot, own, scales,
    s1s, s1r, s2s, s2r, s3s, s3r, s4s, s4r, rss, rsr, fs, fr, *stage,
):
    rows = BLK // CHUNKS
    b, a = lax.axis_index("basis"), lax.axis_index("aux")
    zh, x, c = b // (NX * NCORE), (b // NCORE) % NX, b % NCORE
    zl, y = a // NY, a % NY
    left, right = (y + NY - 1) % NY, (y + 1) % NY

    def at(zh_, x_, c_):
        return (rank(zh_, x_, c_), a)

    def up(y_, zl_=zl):
        return (b, zl_ * NY + y_)

    row_mates = [(dx, dc) for dx in range(NX) for dc in range(NCORE) if dx or dc]
    barrier = pltpu.get_barrier_semaphore()
    mates = [at(zh, (x + dx) % NX, (c + dc) % NCORE) for dx, dc in row_mates]
    mates += [at((zh + d) % NZH, x, c) for d in range(1, NZH)]
    mates += [up(left), up(right), up(y, 1 - zl)]
    for mate in mates:
        pl.semaphore_signal(barrier, inc=1, device_id=mate, device_id_type=MESH)

    pl.semaphore_wait(barrier, len(mates))

    def remote(src, dst, send, recv, mate):
        pltpu.make_async_remote_copy(
            src_ref=src, dst_ref=dst, send_sem=send, recv_sem=recv, device_id=mate, device_id_type=MESH
        ).start()

    for t in range(CHUNKS):
        piece = pl.ds(t * rows, rows)
        for dx, dc in row_mates:
            x_, c_ = (x + dx) % NX, (c + dc) % NCORE
            remote(
                slot.at[piece, pl.ds(pl.multiple_of((4 * c_ + x_) * 128, 128), 128)], stage[t].at[b], s1s.at[t], s1r.at[t], at(zh, x_, c_)
            )
        stage[t][b] = slot[piece, pl.ds(pl.multiple_of((4 * c + x) * 128, 128), 128)]

    def across(t):
        wait_bytes(stage[t].at[pl.ds(0, 7)], s1r.at[t])
        mine = stage[t].at[pl.ds(zh * 8, 8)]
        for d in (1, 3, 2):
            remote(mine, mine, s2s.at[t], s2r.at[t], at((zh + d) % NZH, x, c))

    eighth = 4 * c + x

    def compact(t):
        wait_bytes(stage[t].at[pl.ds(0, 24)], s2r.at[t])
        for j in range(NPB):
            panel[t, eighth, pl.ds(j * rows, rows), :] = stage[t][holders[j]]
        mine = panel.at[t, eighth]
        for d in (1, 3, 2):
            remote(mine, mine, s3s.at[t], s3r.at[t, d - 1], at(zh, (x + d) % NX, c))
        remote(mine, mine, s3s.at[t], s4r.at[t], at(zh, x, 1 - c))

    def share(t):
        for d in (1, 3, 2):
            came = panel.at[t, 4 * c + (x + NX - d) % NX]
            wait_bytes(came, s3r.at[t, d - 1])
            remote(came, came, s4s.at[t], s4r.at[t], at(zh, x, 1 - c))

    def mine_of(t, dest, half):
        return [part[t, g, dest + NY * half] for g in range(LANES)]

    def multiply(t):
        wait_bytes(panel.at[t, pl.ds(0, 4)], s4r.at[t])
        lhs = jnp.concatenate([panel[t, k] for k in range(K8)], axis=1)
        value = lax.dot_general(lhs, kept[...], (((1,), (1,)), ((), ())), preferred_element_type=jnp.float32)
        for g in range(LANES):
            part[t, g] = value[:, g * 128 : (g + 1) * 128].reshape(NPB, rows, 128)
        dest = (y + 4) % NY
        hop_send(t, 0, 0, mine_of(t, dest, 0) * 2)
        hop_send(t, 1, 0, mine_of(t, dest, 1) * 2)

    def hop_send(t, way, step, values):
        count = 4 if step == 0 else 8
        message = sent.at[t, way, step]
        encode(values, rows, scales, message)
        mate = up(right if way == 0 else left)
        remote(message, got.at[t, way, step], rss.at[t, way, step], rsr.at[t, way, step], mate)

    def received(t, way, step):
        wait_bytes(got.at[t, way, step], rsr.at[t, way, step])
        return decode(got.at[t, way, step], rows, 8)

    def hop(t, step):
        for way in range(2):
            dest = (y + 4 - step) % NY if way == 0 else (y + 4 + step) % NY
            came = received(t, way, step - 1)
            half0, half1 = mine_of(t, dest, 0), mine_of(t, dest, 1)
            if step > 1 or way == 0:
                half0 = [p + q for p, q in zip(half0, came[:4])]
            if step > 1 or way == 1:
                half1 = [p + q for p, q in zip(half1, came[4:])]
            hop_send(t, way, step, half0 + half1)

    def merge(t):
        from_left = received(t, 0, 3)
        from_right = received(t, 1, 3)
        for g in range(LANES):
            for half in range(2):
                i = half * 4 + g
                total = part[t, g, y + NY * half] + (from_left[i] + from_right[i])
                own[half, t, g] = total
        fsent[t] = own[1 - zl, t]
        remote(fsent.at[t], fgot.at[t], fs.at[t], fr.at[t], up(y, 1 - zl))

    def finish(t):
        wait_bytes(fgot.at[t], fr.at[t])
        for g in range(LANES):
            out[pl.ds(t * rows, rows), pl.ds(g * 128, 128)] = own[zl, t, g] + fgot[t, g]

    work = {
        "across": across, "compact": compact, "share": share, "multiply": multiply,
        "hop1": lambda t: hop(t, 1), "hop2": lambda t: hop(t, 2), "hop3": lambda t: hop(t, 3),
        "merge": merge, "finish": finish,
    }
    order = sorted((STAGE_AT[s] + SPACING * t, i, t) for i, s in enumerate(work) for t in range(CHUNKS))
    names = list(work)
    for _, i, t in order:
        work[names[i]](t)

    for t in range(CHUNKS):
        wait_bytes(stage[t].at[pl.ds(0, 7)], s1s.at[t])
        wait_bytes(stage[t].at[pl.ds(0, 24)], s2s.at[t])
        wait_bytes(panel.at[t, pl.ds(0, 4)], s3s.at[t])
        wait_bytes(panel.at[t, pl.ds(0, 3)], s4s.at[t])
        for way in range(2):
            for step in range(4):
                wait_bytes(sent.at[t, way, step], rss.at[t, way, step])
        wait_bytes(fsent.at[t], fs.at[t])


def body(half_three, block_mask, panel_blocks):
    cols, auxw, occ = half_three.shape
    nbb, single, nob = block_mask.shape
    width = auxw * occ
    shaped = half_three.reshape(nbb, BLK, auxw, nob, BLK)
    keep = block_mask[:, None, :, :, None].astype(jnp.bfloat16)
    kept = (shaped * keep).reshape(cols, width)
    holders = panel_blocks // nbb
    mine = holders == lax.axis_index("basis")
    within = jnp.sum(jnp.where(mine, panel_blocks % nbb, 0))
    slot = lax.dynamic_slice(kept, (within * BLK, 0), (BLK, width))
    rows = BLK // CHUNKS
    dma = pltpu.SemaphoreType.DMA
    vmem = pltpu.VMEM
    return pl.pallas_call(
        kernel,
        out_shape=jax.ShapeDtypeStruct((BLK, cols), jnp.float32),
        in_specs=[pl.BlockSpec(memory_space=pltpu.VMEM)] * 2 + [pl.BlockSpec(memory_space=pltpu.SMEM)],
        out_specs=pl.BlockSpec(memory_space=pltpu.VMEM),
        scratch_shapes=[
            vmem((CHUNKS, K8, NPB * rows, 128), jnp.bfloat16),
            vmem((CHUNKS, LANES, NPB, rows, 128), jnp.float32),
            vmem((CHUNKS, 2, 4, 8 * rows + 16, 128), jnp.int16),
            vmem((CHUNKS, 2, 4, 8 * rows + 16, 128), jnp.int16),
            vmem((CHUNKS, LANES, rows, 128), jnp.float32),
            vmem((CHUNKS, LANES, rows, 128), jnp.float32),
            vmem((2, CHUNKS, LANES, rows, 128), jnp.float32),
            vmem((8, 128), jnp.float32),
            dma((CHUNKS,)), dma((CHUNKS,)), dma((CHUNKS,)), dma((CHUNKS,)),
            dma((CHUNKS,)), dma((CHUNKS, 3)), dma((CHUNKS,)), dma((CHUNKS,)),
            dma((CHUNKS, 2, 4)), dma((CHUNKS, 2, 4)), dma((CHUNKS,)), dma((CHUNKS,)),
            *[vmem((32, rows, 128), jnp.bfloat16) for _ in range(CHUNKS)],
        ],
        compiler_params=pltpu.CompilerParams(
            collective_id=0, has_side_effects=True, vmem_limit_bytes=56 << 20
        ),
        cost_estimate=pl.CostEstimate(flops=2 * 2048 * cols * width, bytes_accessed=2 << 20, transcendentals=0),
    )(kept, slot, holders)


def solution(mesh):
    placed = (P("basis", "aux", None), P("basis", "aux", None), P())
    return jax.shard_map(
        body, mesh=mesh, in_specs=placed, out_specs=P("aux", "basis"), check_vma=False
    )
```

```python
import functools

import jax
import jax.numpy as jnp
from jax import lax
from jax.experimental import pallas as pl
from jax.experimental.pallas import tpu as pltpu
from jax.sharding import PartitionSpec as P

MESH = pl.DeviceIdType.MESH
NZH, NX, NCORE, NZL, NY = 4, 4, 2, 2, 8
NPB = 16
BLK = 128
K8 = 8
CHUNKS = 8
LANES = 4
TOP = 32767.0
LEVELS = 64.0
LN2 = 0.6931471805599453
AHEAD = {"across": 0, "relay": 4.5, "compact": 8, "share": 11.5, "share2": 15, "multiply": 17}
AFTER = {"hop1": 20.5, "hop2": 24, "hop3": 27.5, "merge": 31, "finish": 34.5}
SPACING = 20.0 / CHUNKS
RELAY_Z = [True] * CHUNKS
RELAY_X = [True] * CHUNKS
STRAIGHT = [t >= CHUNKS - 2 for t in range(CHUNKS)]
HOPS = 4
FULL = sum(4 if straight else 6 for straight in STRAIGHT)
LAST_SLOT = [2 * CHUNKS + sum(5 if s else 1 for s in STRAIGHT[:t]) for t in range(CHUNKS)]
HALF = 2 * CHUNKS + sum(5 if s else 1 for s in STRAIGHT)


def rank(zh, x, c):
    return (zh * NX + x) * NCORE + c


def wait_bytes(view, sem):
    pltpu.make_async_copy(view, view, sem).wait()


def encode(values, rows, scales, message):
    count = len(values)
    for i, value in enumerate(values):
        scales[pl.ds(i, 1), :] = jnp.max(jnp.abs(value), axis=0, keepdims=True)
    most = jnp.maximum(scales[...], 1e-33)
    level = jnp.floor(jnp.log(most) * (LEVELS / LN2)) + 2.0
    factor = jnp.exp(level * (-LN2 / LEVELS)) * TOP
    for i, value in enumerate(values):
        message[pl.ds(i * rows, rows), :] = jnp.round(value * factor[i : i + 1, :]).astype(jnp.int32).astype(jnp.int16)
    both = jnp.concatenate([level, jnp.zeros_like(level)], axis=0)
    message[pl.ds(count * rows, 16), :] = both.astype(jnp.int32).astype(jnp.int16)


def decode(message, rows, count):
    level = message[pl.ds(count * rows, 16), :].astype(jnp.int32).astype(jnp.float32)
    factor = jnp.exp(level * (LN2 / LEVELS)) * (1.0 / TOP)
    return [
        message[pl.ds(i * rows, rows), :].astype(jnp.int32).astype(jnp.float32) * factor[i : i + 1, :]
        for i in range(count)
    ]


def kernel(
    half, mask, blocks, mine_out, came_out, raw, land, kept, slot, panel, part,
    full_sent, full_got, half_sent, half_got, last_got, scales,
    s1s, s1r, s2s, s2n, s2f, s3s, s3n, s3f, s4s, s4r, full_s, half_s, rsr, fr, load, *stage,
):
    rows = BLK // CHUNKS
    b, a = lax.axis_index("basis"), lax.axis_index("aux")
    zh, x, c = b // (NX * NCORE), (b // NCORE) % NX, b % NCORE
    zl, y = a // NY, a % NY
    def at(zh_, x_, c_):
        return (rank(zh_, x_, c_), a)

    def up(y_, zl_=zl):
        return (b, zl_ * NY + y_)

    row_mates = [(dx, dc) for dx in (2, 1, 3, 0) for dc in range(NCORE) if dx or dc]
    barrier = pltpu.get_barrier_semaphore()
    mates = [at((zh + d) % NZH, x, c) for d in ((1, 3) if all(RELAY_Z) else (2, 1, 3))]
    mates += [up((y + d) % NY, 1 - zl) for d in ((1, NY - 1) if any(STRAIGHT) else ())]
    mates += [up((y + d) % NY) for d in (1, NY - 1)] + [up(y, 1 - zl)]
    mates += [at(zh, (x + dx) % NX, (c + dc) % NCORE) for dx, dc in row_mates]
    for mate in mates:
        pl.semaphore_signal(barrier, inc=1, device_id=mate, device_id_type=MESH)

    for w in range(4):
        pltpu.make_async_copy(half.at[pl.ds(w * BLK, BLK)], raw.at[w], load.at[w]).start()
    keeps = [[mask[0, o : o + 1, w : w + 1].astype(jnp.float32) for o in range(2)] for w in range(4)]
    within = jnp.int32(0)
    for j in range(NPB):
        within = within + jnp.where((blocks[j] >> 2) == b, blocks[j] & 3, 0)
    for w in range(4):
        wait_bytes(raw.at[w], load.at[w])

    def masked(block, keep):
        flat = block.reshape(BLK, 1024)
        both = jnp.concatenate([jnp.broadcast_to(k, (1, 128)) for k in keep] * 4, axis=1)
        return flat * both.astype(jnp.bfloat16)

    slot_keep = [sum(jnp.where(within == w, keeps[w][o], 0.0) for w in range(4)) for o in range(2)]
    slot[...] = masked(raw[within], slot_keep)
    pl.semaphore_wait(barrier, len(mates))

    def remote(src, dst, send, recv, mate):
        pltpu.make_async_remote_copy(
            src_ref=src, dst_ref=dst, send_sem=send, recv_sem=recv, device_id=mate, device_id_type=MESH
        ).start()

    eighth = 4 * c + x
    spans = [pl.ds(0, rows), pl.ds(rows, BLK - rows)]
    for i, span in enumerate(spans):
        for dx, dc in row_mates:
            x_, c_ = (x + dx) % NX, (c + dc) % NCORE
            lanes = pl.ds(pl.multiple_of((4 * c_ + x_) * 128, 128), 128)
            remote(slot.at[span, lanes], land.at[x * 2 + c, span], s1s.at[0], s1r.at[i], at(zh, x_, c_))
    land[x * 2 + c] = slot[:, pl.ds(pl.multiple_of(eighth * 128, 128), 128)]
    for w in range(4):
        kept[w] = masked(raw[w], keeps[w])

    def across(t):
        if t < 2:
            wait_bytes(land.at[pl.ds(0, 7), spans[t]], s1r.at[t])
        stage[t][pl.ds(zh * 8, 8)] = land[:, pl.ds(t * rows, rows)]
        mine = stage[t].at[pl.ds(zh * 8, 8)]
        remote(mine, mine, s2s.at[0], s2n.at[t], at((zh + 1) % NZH, x, c))
        remote(mine, mine, s2s.at[0], s2n.at[t], at((zh + 3) % NZH, x, c))
        if not RELAY_Z[t]:
            remote(mine, mine, s2s.at[0], s2f.at[t], at((zh + 2) % NZH, x, c))

    def relay(t):
        wait_bytes(stage[t].at[pl.ds(0, 16)], s2n.at[t])
        for i, d in enumerate((3, 1)):
            origin = ((zh + d) % NZH) * 8
            if RELAY_Z[t]:
                view = stage[t].at[pl.ds(origin + 4 * i, 4)]
                remote(view, view, s2s.at[0], s2f.at[t], at((zh + 4 - d) % NZH, x, c))

    def compact(t):
        wait_bytes(stage[t].at[pl.ds(((zh + 2) % NZH) * 8, 8)], s2f.at[t])
        for j in range(NPB):
            panel[t, eighth, pl.ds(j * rows, rows), :] = stage[t][blocks[j] >> 2]
        mine = panel.at[t, eighth]
        remote(mine, mine, s3s.at[0], s3n.at[t], at(zh, (x + 1) % NX, c))
        remote(mine, mine, s3s.at[0], s3n.at[t], at(zh, (x + 3) % NX, c))
        if not RELAY_X[t]:
            remote(mine, mine, s3s.at[0], s3f.at[t], at(zh, (x + 2) % NX, c))
        remote(mine, mine, s3s.at[0], s4r.at[t], at(zh, x, 1 - c))

    def share(t):
        wait_bytes(panel.at[t, pl.ds(0, 2)], s3n.at[t])
        for i, d in enumerate((3, 1)):
            origin = 4 * c + (x + d) % NX
            came = panel.at[t, origin]
            if RELAY_X[t]:
                view = panel.at[t, origin, pl.ds(8 * rows * i, 8 * rows)]
                remote(view, view, s3s.at[0], s3f.at[t], at(zh, (x + 4 - d) % NX, c))
            remote(came, came, s4s.at[0], s4r.at[t], at(zh, x, 1 - c))

    def share2(t):
        came = panel.at[t, 4 * c + (x + 2) % NX]
        wait_bytes(came, s3f.at[t])
        remote(came, came, s4s.at[0], s4r.at[t], at(zh, x, 1 - c))

    def multiply(t):
        wait_bytes(panel.at[t, pl.ds(0, 4)], s4r.at[t])
        lhs = jnp.concatenate([panel[t, k] for k in range(K8)], axis=1)
        value = lax.dot_general(
            lhs, kept[...].reshape(4 * BLK, 1024), (((1,), (1,)), ((), ())), preferred_element_type=jnp.float32
        )
        for g in range(LANES):
            part[t, g] = value[:, g * 128 : (g + 1) * 128].reshape(NPB, rows, 128)
        hop(t, 0)
        if STRAIGHT[t]:
            send_last(t, 2, 1 - zl, [part[t, g, y + NY * (1 - zl)] for g in range(LANES)])

    def slots(t, step):
        return 2 * t if step == 0 else 2 * (3 * t + step - 1)

    def gathered(t, step, way, halves):
        dest = (y + (HOPS - step) * (1 - 2 * way) + NY) % NY
        total = {(h, g): part[t, g, dest + NY * h] for h in halves for g in range(LANES)}
        if step == 0:
            return total
        for w in (0, 1) if step == HOPS else (way,):
            at_slot = slots(t, step - 1) + w
            message = half_got.at[at_slot] if step == 1 else full_got.at[at_slot]
            came_halves = [w] if step == 1 else [0, 1]
            came = decode(message, rows, LANES * len(came_halves))
            for i, h in enumerate(came_halves):
                for g in range(LANES):
                    total[h, g] = total[h, g] + came[i * LANES + g]
        return total

    def arrive(t, step):
        got = half_got if step == 0 else full_got
        wait_bytes(got.at[pl.ds(slots(t, step), 2)], rsr.at[t, step])

    def hop(t, step):
        if step:
            arrive(t, step - 1)
        for way in range(2):
            total = gathered(t, step, way, [way] if step == 0 else [0, 1])
            values = [v for _, v in sorted(total.items())]
            mate_y = (y + (1 if way == 0 else NY - 1)) % NY
            if step == HOPS - 1 and STRAIGHT[t]:
                for h in range(2):
                    send_last(t, way, h, values[LANES * h : LANES * h + LANES], mate_y)
                continue
            sent, got, sem = (half_sent, half_got, half_s) if step == 0 else (full_sent, full_got, full_s)
            at_slot = slots(t, step) + way
            encode(values, rows, scales, sent.at[at_slot])
            remote(sent.at[at_slot], got.at[at_slot], sem.at[0], rsr.at[t, step], up(mate_y))

    def send_last(t, way, h, values, mate_y=None):
        to = y if mate_y is None else mate_y
        at_slot = 4 if way == 2 else way + 2 * ((h + zl) % 2)
        number = LAST_SLOT[t] + (4 if way == 2 else way + 2 * h)
        message = half_sent.at[number]
        encode(values, rows, scales, message)
        remote(message, last_got.at[t, at_slot], half_s.at[0], fr.at[t], up(to, h))

    def merge(t):
        if STRAIGHT[t]:
            wait_bytes(last_got.at[t], fr.at[t])
            for g in range(LANES):
                mine_out[pl.ds(t * rows, rows), pl.ds(g * 128, 128)] = part[t, g, y + NY * zl]
            came = [decode(last_got.at[t, i], rows, LANES) for i in range(5)]
            for g in range(LANES):
                came_out[pl.ds(t * rows, rows), pl.ds(g * 128, 128)] = sum(part_[g] for part_ in came)
            return
        arrive(t, HOPS - 1)
        total = gathered(t, HOPS, 0, [0, 1])
        away = [jnp.where(zl == 0, total[1, g], total[0, g]) for g in range(LANES)]
        for g in range(LANES):
            lanes = pl.ds(g * 128, 128)
            mine_out[pl.ds(t * rows, rows), lanes] = jnp.where(zl == 0, total[0, g], total[1, g])
        message = half_sent.at[LAST_SLOT[t]]
        encode(away, rows, scales, message)
        remote(message, last_got.at[t, 4], half_s.at[0], fr.at[t], up(y, 1 - zl))

    def finish(t):
        if STRAIGHT[t]:
            return
        wait_bytes(last_got.at[t, 4], fr.at[t])
        for g, value in enumerate(decode(last_got.at[t, 4], rows, LANES)):
            came_out[pl.ds(t * rows, rows), pl.ds(g * 128, 128)] = value

    work = {
        "across": across, "relay": relay, "compact": compact, "share": share, "share2": share2, "multiply": multiply,
        "hop1": lambda t: hop(t, 1), "hop2": lambda t: hop(t, 2), "hop3": lambda t: hop(t, 3),
        "merge": merge, "finish": finish,
    }
    when = []
    for t in range(CHUNKS):
        plan = AHEAD | AFTER
        when += [(plan[name] + SPACING * t, i, t, name) for i, name in enumerate(work)]
    for _, _, t, name in sorted(when):
        work[name](t)

    wait_bytes(land.at[pl.ds(0, 7)], s1s.at[0])
    wait_bytes(panel.at[pl.ds(0, CHUNKS // 2), pl.ds(0, 3)], s2s.at[0])
    wait_bytes(panel.at[:, pl.ds(0, 4)], s3s.at[0])
    wait_bytes(panel.at[:, pl.ds(0, 3)], s4s.at[0])
    wait_bytes(full_sent.at[pl.ds(0, FULL)], full_s.at[0])
    wait_bytes(half_sent, half_s.at[0])


def body(half_three, block_mask, panel_blocks):
    cols, auxw, occ = half_three.shape
    width = auxw * occ
    rows = BLK // CHUNKS
    dma = pltpu.SemaphoreType.DMA
    vmem = pltpu.VMEM
    mine, came = pl.pallas_call(
        kernel,
        out_shape=[jax.ShapeDtypeStruct((BLK, cols), jnp.float32)] * 2,
        in_specs=[
            pl.BlockSpec(memory_space=pltpu.HBM),
            pl.BlockSpec(memory_space=pltpu.VMEM),
            pl.BlockSpec(memory_space=pltpu.SMEM),
        ],
        out_specs=[pl.BlockSpec(memory_space=pltpu.VMEM)] * 2,
        scratch_shapes=[
            vmem((4, BLK, auxw, occ), jnp.bfloat16),
            vmem((8, BLK, 128), jnp.bfloat16),
            vmem((4, BLK, width), jnp.bfloat16),
            vmem((BLK, width), jnp.bfloat16),
            vmem((CHUNKS, K8, NPB * rows, 128), jnp.bfloat16),
            vmem((CHUNKS, LANES, NPB, rows, 128), jnp.float32),
            vmem((6 * CHUNKS, 8 * rows + 16, 128), jnp.int16),
            vmem((6 * CHUNKS, 8 * rows + 16, 128), jnp.int16),
            vmem((HALF, 4 * rows + 16, 128), jnp.int16),
            vmem((2 * CHUNKS, 4 * rows + 16, 128), jnp.int16),
            vmem((CHUNKS, 5, 4 * rows + 16, 128), jnp.int16),
            vmem((8, 128), jnp.float32),
            dma((1,)), dma((2,)), dma((1,)), dma((CHUNKS,)), dma((CHUNKS,)),
            dma((1,)), dma((CHUNKS,)), dma((CHUNKS,)), dma((1,)), dma((CHUNKS,)),
            dma((1,)), dma((1,)), dma((CHUNKS, HOPS)), dma((CHUNKS,)), dma((4,)),
            *[vmem((32, rows, 128), jnp.bfloat16) for _ in range(CHUNKS)],
        ],
        compiler_params=pltpu.CompilerParams(
            collective_id=0, has_side_effects=True, vmem_limit_bytes=24 << 20
        ),
        cost_estimate=pl.CostEstimate(flops=2 * 2048 * cols * width, bytes_accessed=2 << 20, transcendentals=0),
    )(half_three, block_mask.transpose(1, 2, 0), panel_blocks)
    return mine + came


def solution(mesh):
    placed = (P("basis", "aux", None), P("basis", "aux", None), P())
    return jax.shard_map(
        body, mesh=mesh, in_specs=placed, out_specs=P("aux", "basis"), check_vma=False
    )
```

```python
import functools

import jax
import jax.numpy as jnp
from jax import lax
from jax.experimental import pallas as pl
from jax.experimental.pallas import tpu as pltpu
from jax.sharding import PartitionSpec as P

MESH = pl.DeviceIdType.MESH
NZH, NX, NCORE, NZL, NY = 4, 4, 2, 2, 8
NPB = 16
BLK = 128
K8 = 8
CHUNKS = 8
LANES = 4
TOP = 32767.0
AHEAD = {"across": 0, "relay": 4.5, "compact": 8, "share": 11.5, "share2": 15, "multiply": 17}
AFTER = {"hop1": 20.5, "hop2": 24, "hop3": 27.5, "merge": 31, "finish": 34.5}
SPACING = 14.0 / CHUNKS
RELAY_Z = [True] * CHUNKS
RELAY_X = [t > 0 for t in range(CHUNKS)]
STRAIGHT = [t >= CHUNKS - 2 for t in range(CHUNKS)]
HOPS = 4
FULL = sum(4 if straight else 6 for straight in STRAIGHT)
FULL_SLOT = [sum(4 if s else 6 for s in STRAIGHT[:t]) for t in range(CHUNKS)]
LAST_SLOT = [2 * CHUNKS + sum(5 if s else 1 for s in STRAIGHT[:t]) for t in range(CHUNKS)]
HALF = 2 * CHUNKS + sum(5 if s else 1 for s in STRAIGHT)


def rank(zh, x, c):
    return (zh * NX + x) * NCORE + c


def wait_bytes(view, sem):
    pltpu.make_async_copy(view, view, sem).wait()


def encode(values, rows, message, scale):
    for n in range(0, len(values), LANES):
        block = values[n : n + LANES]
        most = functools.reduce(jnp.maximum, [jnp.abs(value) for value in block])
        most = jnp.maximum(jnp.max(most, axis=0, keepdims=True), 1e-33)
        scale[n // LANES] = most
        factor = TOP / most
        for i, value in enumerate(block):
            coded = jnp.round(value * factor).astype(jnp.int32).astype(jnp.int16)
            message[pl.ds((n + i) * rows, rows), :] = coded


def decode(message, scale, rows, count):
    factors = [scale[n] * (1.0 / TOP) for n in range(count // LANES)]
    return [
        message[pl.ds(i * rows, rows), :].astype(jnp.int32).astype(jnp.float32) * factors[i // LANES]
        for i in range(count)
    ]


def kernel(
    half, mask, blocks, mine_out, came_out, raw, land, kept, slot, panel, part,
    full_sent, full_got, half_sent, half_got, last_got,
    scale_sent, full_scale, half_scale, last_scale, tally,
    s1s, s1r, s2s, s2n, s2f, s3s, s3n, s3f, s4s, s4r, full_s, half_s, scale_s, rsr, fr, load, *stage,
):
    rows = BLK // CHUNKS
    b, a = lax.axis_index("basis"), lax.axis_index("aux")
    zh, x, c = b // (NX * NCORE), (b // NCORE) % NX, b % NCORE
    zl, y = a // NY, a % NY
    def at(zh_, x_, c_):
        return (rank(zh_, x_, c_), a)

    def up(y_, zl_=zl):
        return (b, zl_ * NY + y_)

    row_mates = [(dx, dc) for dx in (2, 1, 3, 0) for dc in range(NCORE) if dx or dc]
    barrier = pltpu.get_barrier_semaphore()
    mates = [at((zh + d) % NZH, x, c) for d in ((1, 3) if all(RELAY_Z) else (2, 1, 3))]
    mates += [up((y + d) % NY, 1 - zl) for d in ((1, NY - 1) if any(STRAIGHT) else ())]
    mates += [up((y + d) % NY) for d in (1, NY - 1)] + [up(y, 1 - zl)]
    mates += [at(zh, (x + dx) % NX, (c + dc) % NCORE) for dx, dc in row_mates]
    for mate in mates:
        pl.semaphore_signal(barrier, inc=1, device_id=mate, device_id_type=MESH)

    for w in range(4):
        pltpu.make_async_copy(half.at[pl.ds(w * BLK, BLK)], raw.at[w], load.at[w]).start()
    keeps = [[mask[0, o : o + 1, w : w + 1].astype(jnp.float32) for o in range(2)] for w in range(4)]
    within = jnp.int32(0)
    for j in range(NPB):
        within = within + jnp.where((blocks[j] >> 2) == b, blocks[j] & 3, 0)
    for w in range(4):
        wait_bytes(raw.at[w], load.at[w])

    def masked(block, keep):
        flat = block.reshape(BLK, 1024)
        both = jnp.concatenate([jnp.broadcast_to(k, (1, 128)) for k in keep] * 4, axis=1)
        return flat * both.astype(jnp.bfloat16)

    slot_keep = [sum(jnp.where(within == w, keeps[w][o], 0.0) for w in range(4)) for o in range(2)]
    slot[...] = masked(raw[within], slot_keep)
    pl.semaphore_wait(barrier, len(mates))

    def remote(src, dst, send, recv, mate):
        pltpu.make_async_remote_copy(
            src_ref=src, dst_ref=dst, send_sem=send, recv_sem=recv, device_id=mate, device_id_type=MESH
        ).start()

    eighth = 4 * c + x
    spans = [pl.ds(0, rows), pl.ds(rows, BLK - rows)]
    for i, span in enumerate(spans):
        for dx, dc in row_mates:
            x_, c_ = (x + dx) % NX, (c + dc) % NCORE
            lanes = pl.ds(pl.multiple_of((4 * c_ + x_) * 128, 128), 128)
            remote(slot.at[span, lanes], land.at[x * 2 + c, span], s1s.at[0], s1r.at[i], at(zh, x_, c_))
    land[x * 2 + c] = slot[:, pl.ds(pl.multiple_of(eighth * 128, 128), 128)]
    for w in range(4):
        kept[w] = masked(raw[w], keeps[w])

    def across(t):
        if t < 2:
            wait_bytes(land.at[pl.ds(0, 7), spans[t]], s1r.at[t])
        stage[t][pl.ds(zh * 8, 8)] = land[:, pl.ds(t * rows, rows)]
        mine = stage[t].at[pl.ds(zh * 8, 8)]
        remote(mine, mine, s2s.at[0], s2n.at[t], at((zh + 1) % NZH, x, c))
        remote(mine, mine, s2s.at[0], s2n.at[t], at((zh + 3) % NZH, x, c))
        if not RELAY_Z[t]:
            remote(mine, mine, s2s.at[0], s2f.at[t], at((zh + 2) % NZH, x, c))

    def relay(t):
        wait_bytes(stage[t].at[pl.ds(0, 16)], s2n.at[t])
        for i, d in enumerate((3, 1)):
            origin = ((zh + d) % NZH) * 8
            if RELAY_Z[t]:
                view = stage[t].at[pl.ds(origin + 4 * i, 4)]
                remote(view, view, s2s.at[0], s2f.at[t], at((zh + 4 - d) % NZH, x, c))

    def compact(t):
        wait_bytes(stage[t].at[pl.ds(((zh + 2) % NZH) * 8, 8)], s2f.at[t])
        for j in range(NPB):
            panel[t, eighth, pl.ds(j * rows, rows), :] = stage[t][blocks[j] >> 2]
        mine = panel.at[t, eighth]
        remote(mine, mine, s3s.at[0], s3n.at[t], at(zh, (x + 1) % NX, c))
        remote(mine, mine, s3s.at[0], s3n.at[t], at(zh, (x + 3) % NX, c))
        if not RELAY_X[t]:
            remote(mine, mine, s3s.at[0], s3f.at[t], at(zh, (x + 2) % NX, c))
        remote(mine, mine, s3s.at[0], s4r.at[t], at(zh, x, 1 - c))

    def share(t):
        wait_bytes(panel.at[t, pl.ds(0, 2)], s3n.at[t])
        for i, d in enumerate((3, 1)):
            origin = 4 * c + (x + d) % NX
            came = panel.at[t, origin]
            if RELAY_X[t]:
                view = panel.at[t, origin, pl.ds(8 * rows * i, 8 * rows)]
                remote(view, view, s3s.at[0], s3f.at[t], at(zh, (x + 4 - d) % NX, c))
            remote(came, came, s4s.at[0], s4r.at[t], at(zh, x, 1 - c))

    def share2(t):
        came = panel.at[t, 4 * c + (x + 2) % NX]
        wait_bytes(came, s3f.at[t])
        remote(came, came, s4s.at[0], s4r.at[t], at(zh, x, 1 - c))

    def multiply(t):
        wait_bytes(panel.at[t, pl.ds(0, 4)], s4r.at[t])
        lhs = jnp.concatenate([panel[t, k] for k in range(K8)], axis=1)
        value = lax.dot_general(
            lhs, kept[...].reshape(4 * BLK, 1024), (((1,), (1,)), ((), ())), preferred_element_type=jnp.float32
        )
        for g in range(LANES):
            part[t, g] = value[:, g * 128 : (g + 1) * 128].reshape(NPB, rows, 128)
        hop(t, 0)
        if STRAIGHT[t]:
            send_last(t, 2, 1 - zl, [part[t, g, y + NY * (1 - zl)] for g in range(LANES)])

    full_rows, half_rows = 4 * rows + 2, 2 * rows + 1

    def slots(t, step):
        return 2 * t if step == 0 else FULL_SLOT[t] + 2 * (step - 1)

    def gathered(t, step, way, halves):
        dest = (y + (HOPS - step) * (1 - 2 * way) + NY) % NY
        total = {(h, g): part[t, g, dest + NY * h] for h in halves for g in range(LANES)}
        if step == 0:
            return total
        for w in (0, 1) if step == HOPS else (way,):
            at_slot = slots(t, step - 1) + w
            got, scale = (half_got, half_scale) if step == 1 else (full_got, full_scale)
            came_halves = [w] if step == 1 else [0, 1]
            came = decode(got.at[at_slot], scale.at[at_slot], rows, LANES * len(came_halves))
            for i, h in enumerate(came_halves):
                for g in range(LANES):
                    total[h, g] = total[h, g] + came[i * LANES + g]
        return total

    def arrive(t, step):
        wait_bytes(tally.at[pl.ds(0, 2 * (half_rows if step == 0 else full_rows))], rsr.at[t, step])

    def hop(t, step):
        if step:
            arrive(t, step - 1)
        for way in range(2):
            total = gathered(t, step, way, [way] if step == 0 else [0, 1])
            values = [v for _, v in sorted(total.items())]
            mate_y = (y + (1 if way == 0 else NY - 1)) % NY
            if step == HOPS - 1 and STRAIGHT[t]:
                for h in range(2):
                    send_last(t, way, h, values[LANES * h : LANES * h + LANES], mate_y)
                continue
            at_slot = slots(t, step) + way
            if step == 0:
                send(values, half_sent.at[at_slot], pl.ds(2 * FULL + at_slot, 1), half_got, half_scale, at_slot, half_s, rsr.at[t, step], up(mate_y))
            else:
                send(values, full_sent.at[at_slot], pl.ds(2 * at_slot, 2), full_got, full_scale, at_slot, full_s, rsr.at[t, step], up(mate_y))

    def send(values, message, number, got, got_scale, where, sem, recv, mate):
        encode(values, rows, message, scale_sent.at[number])
        remote(message, got.at[where], sem.at[0], recv, mate)
        remote(scale_sent.at[number], got_scale.at[where], scale_s.at[0], recv, mate)

    def send_last(t, way, h, values, mate_y=None):
        to = y if mate_y is None else mate_y
        at_slot = 4 if way == 2 else way + 2 * ((h + zl) % 2)
        number = LAST_SLOT[t] + (4 if way == 2 else way + 2 * h)
        send(values, half_sent.at[number], pl.ds(2 * FULL + number, 1), last_got.at[t], last_scale.at[t], at_slot, half_s, fr.at[t], up(to, h))

    def merge(t):
        if STRAIGHT[t]:
            wait_bytes(tally.at[pl.ds(0, 5 * half_rows)], fr.at[t])
            for g in range(LANES):
                mine_out[pl.ds(t * rows, rows), pl.ds(g * 128, 128)] = part[t, g, y + NY * zl]
            came = [decode(last_got.at[t, i], last_scale.at[t, i], rows, LANES) for i in range(5)]
            for g in range(LANES):
                came_out[pl.ds(t * rows, rows), pl.ds(g * 128, 128)] = sum(part_[g] for part_ in came)
            return
        arrive(t, HOPS - 1)
        total = gathered(t, HOPS, 0, [0, 1])
        away = [jnp.where(zl == 0, total[1, g], total[0, g]) for g in range(LANES)]
        for g in range(LANES):
            lanes = pl.ds(g * 128, 128)
            mine_out[pl.ds(t * rows, rows), lanes] = jnp.where(zl == 0, total[0, g], total[1, g])
        number = LAST_SLOT[t]
        send(away, half_sent.at[number], pl.ds(2 * FULL + number, 1), last_got.at[t], last_scale.at[t], 4, half_s, fr.at[t], up(y, 1 - zl))

    def finish(t):
        if STRAIGHT[t]:
            return
        wait_bytes(tally.at[pl.ds(0, half_rows)], fr.at[t])
        for g, value in enumerate(decode(last_got.at[t, 4], last_scale.at[t, 4], rows, LANES)):
            came_out[pl.ds(t * rows, rows), pl.ds(g * 128, 128)] = value

    work = {
        "across": across, "relay": relay, "compact": compact, "share": share, "share2": share2, "multiply": multiply,
        "hop1": lambda t: hop(t, 1), "hop2": lambda t: hop(t, 2), "hop3": lambda t: hop(t, 3),
        "merge": merge, "finish": finish,
    }
    when = []
    for t in range(CHUNKS):
        plan = AHEAD | AFTER
        when += [(plan[name] + SPACING * t, i, t, name) for i, name in enumerate(work)]
    for _, _, t, name in sorted(when):
        work[name](t)

    wait_bytes(land.at[pl.ds(0, 7)], s1s.at[0])
    wait_bytes(panel.at[pl.ds(0, CHUNKS // 2), pl.ds(0, 3)], s2s.at[0])
    wait_bytes(panel.at[:, pl.ds(0, 4)], s3s.at[0])
    wait_bytes(panel.at[:, pl.ds(0, 3)], s4s.at[0])
    wait_bytes(full_sent, full_s.at[0])
    wait_bytes(half_sent, half_s.at[0])
    wait_bytes(scale_sent, scale_s.at[0])


def body(half_three, block_mask, panel_blocks):
    cols, auxw, occ = half_three.shape
    width = auxw * occ
    rows = BLK // CHUNKS
    dma = pltpu.SemaphoreType.DMA
    vmem = pltpu.VMEM
    mine, came = pl.pallas_call(
        kernel,
        out_shape=[jax.ShapeDtypeStruct((BLK, cols), jnp.float32)] * 2,
        in_specs=[
            pl.BlockSpec(memory_space=pltpu.HBM),
            pl.BlockSpec(memory_space=pltpu.VMEM),
            pl.BlockSpec(memory_space=pltpu.SMEM),
        ],
        out_specs=[pl.BlockSpec(memory_space=pltpu.VMEM)] * 2,
        scratch_shapes=[
            vmem((4, BLK, auxw, occ), jnp.bfloat16),
            vmem((8, BLK, 128), jnp.bfloat16),
            vmem((4, BLK, width), jnp.bfloat16),
            vmem((BLK, width), jnp.bfloat16),
            vmem((CHUNKS, K8, NPB * rows, 128), jnp.bfloat16),
            vmem((CHUNKS, LANES, NPB, rows, 128), jnp.float32),
            vmem((FULL, 8 * rows, 128), jnp.int16),
            vmem((FULL, 8 * rows, 128), jnp.int16),
            vmem((HALF, 4 * rows, 128), jnp.int16),
            vmem((2 * CHUNKS, 4 * rows, 128), jnp.int16),
            vmem((CHUNKS, 5, 4 * rows, 128), jnp.int16),
            vmem((2 * FULL + HALF, 1, 128), jnp.float32),
            vmem((FULL, 2, 1, 128), jnp.float32),
            vmem((2 * CHUNKS, 1, 1, 128), jnp.float32),
            vmem((CHUNKS, 5, 1, 1, 128), jnp.float32),
            vmem((5 * (2 * rows + 1), 1, 128), jnp.float32),
            dma((1,)), dma((2,)), dma((1,)), dma((CHUNKS,)), dma((CHUNKS,)),
            dma((1,)), dma((CHUNKS,)), dma((CHUNKS,)), dma((1,)), dma((CHUNKS,)),
            dma((1,)), dma((1,)), dma((1,)), dma((CHUNKS, HOPS)), dma((CHUNKS,)), dma((4,)),
            *[vmem((32, rows, 128), jnp.bfloat16) for _ in range(CHUNKS)],
        ],
        compiler_params=pltpu.CompilerParams(
            collective_id=0, has_side_effects=True, vmem_limit_bytes=24 << 20
        ),
        cost_estimate=pl.CostEstimate(flops=2 * 2048 * cols * width, bytes_accessed=2 << 20, transcendentals=0),
    )(half_three, block_mask.transpose(1, 2, 0), panel_blocks)
    return mine + came


def solution(mesh):
    placed = (P("basis", "aux", None), P("basis", "aux", None), P())
    return jax.shard_map(
        body, mesh=mesh, in_specs=placed, out_specs=P("aux", "basis"), check_vma=False
    )
```

```python
import functools

import jax
import jax.numpy as jnp
from jax import lax
from jax.experimental import pallas as pl
from jax.experimental.pallas import tpu as pltpu
from jax.sharding import PartitionSpec as P

MESH = pl.DeviceIdType.MESH
NZH, NX, NCORE, NZL, NY = 4, 4, 2, 2, 8
NPB = 16
BLK = 128
K8 = 8
CHUNKS = 8
LANES = 4
TOP = 32767.0
AHEAD = {"across": 0, "relay": 4.5, "compact": 8, "share": 11.5, "share2": 15, "multiply": 17}
AFTER = {"hop1": 20.5, "hop2": 24, "hop3": 27.5, "merge": 31, "finish": 34.5}
SPACING = 14.0 / CHUNKS
RELAY_Z = [True] * CHUNKS
RELAY_X = [t > 0 for t in range(CHUNKS)]
STRAIGHT = [t >= CHUNKS - 2 for t in range(CHUNKS)]
HOPS = 4
FULL = sum(4 if straight else 6 for straight in STRAIGHT)
FULL_SLOT = [sum(4 if s else 6 for s in STRAIGHT[:t]) for t in range(CHUNKS)]
LAST_SLOT = [2 * CHUNKS + sum(5 if s else 1 for s in STRAIGHT[:t]) for t in range(CHUNKS)]
HALF = 2 * CHUNKS + sum(5 if s else 1 for s in STRAIGHT)


def rank(zh, x, c):
    return (zh * NX + x) * NCORE + c


def wait_bytes(view, sem):
    pltpu.make_async_copy(view, view, sem).wait()


def encode(values, rows, message, scale):
    for n in range(0, len(values), LANES):
        block = values[n : n + LANES]
        most = functools.reduce(jnp.maximum, [jnp.abs(value) for value in block])
        most = jnp.maximum(jnp.max(most, axis=0, keepdims=True), 1e-33)
        scale[n // LANES] = most
        factor = TOP / most
        for i, value in enumerate(block):
            coded = jnp.round(value * factor).astype(jnp.int32).astype(jnp.int16)
            message[pl.ds((n + i) * rows, rows), :] = coded


def decode(message, scale, rows, count):
    factors = [scale[n] * (1.0 / TOP) for n in range(count // LANES)]
    return [
        message[pl.ds(i * rows, rows), :].astype(jnp.int32).astype(jnp.float32) * factors[i // LANES]
        for i in range(count)
    ]


def kernel(
    half, mask_in, blocks_in, mine_out, came_out, raw, land, kept, slot, panel, part,
    full_sent, full_got, half_sent, half_got, last_got,
    scale_sent, full_scale, half_scale, last_scale, tally,
    s1s, s1r, s2s, s2n, s2f, s3s, s3n, s3f, s4s, s4r, full_s, half_s, scale_s, rsr, fr, load, mask, blocks, *stage,
):
    rows = BLK // CHUNKS
    b, a = lax.axis_index("basis"), lax.axis_index("aux")
    zh, x, c = b // (NX * NCORE), (b // NCORE) % NX, b % NCORE
    zl, y = a // NY, a % NY
    def at(zh_, x_, c_):
        return (rank(zh_, x_, c_), a)

    def up(y_, zl_=zl):
        return (b, zl_ * NY + y_)

    row_mates = [(dx, dc) for dx in (2, 1, 3, 0) for dc in range(NCORE) if dx or dc]
    barrier = pltpu.get_barrier_semaphore()
    mates = [at((zh + d) % NZH, x, c) for d in ((1, 3) if all(RELAY_Z) else (2, 1, 3))]
    mates += [up((y + d) % NY, 1 - zl) for d in ((1, NY - 1) if any(STRAIGHT) else ())]
    mates += [up((y + d) % NY) for d in (1, NY - 1)] + [up(y, 1 - zl)]
    mates += [at(zh, (x + dx) % NX, (c + dc) % NCORE) for dx, dc in row_mates]
    for mate in mates:
        pl.semaphore_signal(barrier, inc=1, device_id=mate, device_id_type=MESH)

    small = [pltpu.make_async_copy(mask_in, mask, load.at[4]), pltpu.make_async_copy(blocks_in, blocks, load.at[5])]
    for copy in small:
        copy.start()
    for w in range(4):
        pltpu.make_async_copy(half.at[pl.ds(w * BLK, BLK)], raw.at[w], load.at[w]).start()
    for copy in small:
        copy.wait()
    keeps = [[mask[0, o : o + 1, w : w + 1].astype(jnp.float32) for o in range(2)] for w in range(4)]
    within = jnp.int32(0)
    for j in range(NPB):
        within = within + jnp.where((blocks[j] >> 2) == b, blocks[j] & 3, 0)
    for w in range(4):
        wait_bytes(raw.at[w], load.at[w])

    def masked(block, keep):
        flat = block.reshape(BLK, 1024)
        both = jnp.concatenate([jnp.broadcast_to(k, (1, 128)) for k in keep] * 4, axis=1)
        return flat * both.astype(jnp.bfloat16)

    slot_keep = [sum(jnp.where(within == w, keeps[w][o], 0.0) for w in range(4)) for o in range(2)]
    slot[...] = masked(raw[within], slot_keep)
    pl.semaphore_wait(barrier, len(mates))

    def remote(src, dst, send, recv, mate):
        pltpu.make_async_remote_copy(
            src_ref=src, dst_ref=dst, send_sem=send, recv_sem=recv, device_id=mate, device_id_type=MESH
        ).start()

    eighth = 4 * c + x
    spans = [pl.ds(0, rows), pl.ds(rows, BLK - rows)]
    for i, span in enumerate(spans):
        for dx, dc in row_mates:
            x_, c_ = (x + dx) % NX, (c + dc) % NCORE
            lanes = pl.ds(pl.multiple_of((4 * c_ + x_) * 128, 128), 128)
            remote(slot.at[span, lanes], land.at[x * 2 + c, span], s1s.at[0], s1r.at[i], at(zh, x_, c_))
    land[x * 2 + c] = slot[:, pl.ds(pl.multiple_of(eighth * 128, 128), 128)]
    for w in range(4):
        kept[w] = masked(raw[w], keeps[w])

    def across(t):
        if t < 2:
            wait_bytes(land.at[pl.ds(0, 7), spans[t]], s1r.at[t])
        stage[t][pl.ds(zh * 8, 8)] = land[:, pl.ds(t * rows, rows)]
        mine = stage[t].at[pl.ds(zh * 8, 8)]
        remote(mine, mine, s2s.at[0], s2n.at[t], at((zh + 1) % NZH, x, c))
        remote(mine, mine, s2s.at[0], s2n.at[t], at((zh + 3) % NZH, x, c))
        if not RELAY_Z[t]:
            remote(mine, mine, s2s.at[0], s2f.at[t], at((zh + 2) % NZH, x, c))

    def relay(t):
        wait_bytes(stage[t].at[pl.ds(0, 16)], s2n.at[t])
        for i, d in enumerate((3, 1)):
            origin = ((zh + d) % NZH) * 8
            if RELAY_Z[t]:
                view = stage[t].at[pl.ds(origin + 4 * i, 4)]
                remote(view, view, s2s.at[0], s2f.at[t], at((zh + 4 - d) % NZH, x, c))

    def compact(t):
        wait_bytes(stage[t].at[pl.ds(((zh + 2) % NZH) * 8, 8)], s2f.at[t])
        for j in range(NPB):
            panel[t, eighth, pl.ds(j * rows, rows), :] = stage[t][blocks[j] >> 2]
        mine = panel.at[t, eighth]
        remote(mine, mine, s3s.at[0], s3n.at[t], at(zh, (x + 1) % NX, c))
        remote(mine, mine, s3s.at[0], s3n.at[t], at(zh, (x + 3) % NX, c))
        if not RELAY_X[t]:
            remote(mine, mine, s3s.at[0], s3f.at[t], at(zh, (x + 2) % NX, c))
        remote(mine, mine, s3s.at[0], s4r.at[t], at(zh, x, 1 - c))

    def share(t):
        wait_bytes(panel.at[t, pl.ds(0, 2)], s3n.at[t])
        for i, d in enumerate((3, 1)):
            origin = 4 * c + (x + d) % NX
            came = panel.at[t, origin]
            if RELAY_X[t]:
                view = panel.at[t, origin, pl.ds(8 * rows * i, 8 * rows)]
                remote(view, view, s3s.at[0], s3f.at[t], at(zh, (x + 4 - d) % NX, c))
            remote(came, came, s4s.at[0], s4r.at[t], at(zh, x, 1 - c))

    def share2(t):
        came = panel.at[t, 4 * c + (x + 2) % NX]
        wait_bytes(came, s3f.at[t])
        remote(came, came, s4s.at[0], s4r.at[t], at(zh, x, 1 - c))

    def multiply(t):
        wait_bytes(panel.at[t, pl.ds(0, 4)], s4r.at[t])
        lhs = jnp.concatenate([panel[t, k] for k in range(K8)], axis=1)
        value = lax.dot_general(
            lhs, kept[...].reshape(4 * BLK, 1024), (((1,), (1,)), ((), ())), preferred_element_type=jnp.float32
        )
        for g in range(LANES):
            part[t, g] = value[:, g * 128 : (g + 1) * 128].reshape(NPB, rows, 128)
        hop(t, 0)
        if STRAIGHT[t]:
            send_last(t, 2, 1 - zl, [part[t, g, y + NY * (1 - zl)] for g in range(LANES)])

    full_rows, half_rows = 4 * rows + 2, 2 * rows + 1

    def slots(t, step):
        return 2 * t if step == 0 else FULL_SLOT[t] + 2 * (step - 1)

    def gathered(t, step, way, halves):
        dest = (y + (HOPS - step) * (1 - 2 * way) + NY) % NY
        total = {(h, g): part[t, g, dest + NY * h] for h in halves for g in range(LANES)}
        if step == 0:
            return total
        for w in (0, 1) if step == HOPS else (way,):
            at_slot = slots(t, step - 1) + w
            got, scale = (half_got, half_scale) if step == 1 else (full_got, full_scale)
            came_halves = [w] if step == 1 else [0, 1]
            came = decode(got.at[at_slot], scale.at[at_slot], rows, LANES * len(came_halves))
            for i, h in enumerate(came_halves):
                for g in range(LANES):
                    total[h, g] = total[h, g] + came[i * LANES + g]
        return total

    def arrive(t, step):
        wait_bytes(tally.at[pl.ds(0, 2 * (half_rows if step == 0 else full_rows))], rsr.at[t, step])

    def hop(t, step):
        if step:
            arrive(t, step - 1)
        for way in range(2):
            total = gathered(t, step, way, [way] if step == 0 else [0, 1])
            values = [v for _, v in sorted(total.items())]
            mate_y = (y + (1 if way == 0 else NY - 1)) % NY
            if step == HOPS - 1 and STRAIGHT[t]:
                for h in range(2):
                    send_last(t, way, h, values[LANES * h : LANES * h + LANES], mate_y)
                continue
            at_slot = slots(t, step) + way
            if step == 0:
                send(values, half_sent.at[at_slot], pl.ds(2 * FULL + at_slot, 1), half_got, half_scale, at_slot, half_s, rsr.at[t, step], up(mate_y))
            else:
                send(values, full_sent.at[at_slot], pl.ds(2 * at_slot, 2), full_got, full_scale, at_slot, full_s, rsr.at[t, step], up(mate_y))

    def send(values, message, number, got, got_scale, where, sem, recv, mate):
        encode(values, rows, message, scale_sent.at[number])
        remote(message, got.at[where], sem.at[0], recv, mate)
        remote(scale_sent.at[number], got_scale.at[where], scale_s.at[0], recv, mate)

    def send_last(t, way, h, values, mate_y=None):
        to = y if mate_y is None else mate_y
        at_slot = 4 if way == 2 else way + 2 * ((h + zl) % 2)
        number = LAST_SLOT[t] + (4 if way == 2 else way + 2 * h)
        send(values, half_sent.at[number], pl.ds(2 * FULL + number, 1), last_got.at[t], last_scale.at[t], at_slot, half_s, fr.at[t], up(to, h))

    def merge(t):
        if STRAIGHT[t]:
            wait_bytes(tally.at[pl.ds(0, 5 * half_rows)], fr.at[t])
            for g in range(LANES):
                mine_out[pl.ds(t * rows, rows), pl.ds(g * 128, 128)] = part[t, g, y + NY * zl]
            came = [decode(last_got.at[t, i], last_scale.at[t, i], rows, LANES) for i in range(5)]
            for g in range(LANES):
                came_out[pl.ds(t * rows, rows), pl.ds(g * 128, 128)] = sum(part_[g] for part_ in came)
            return
        arrive(t, HOPS - 1)
        total = gathered(t, HOPS, 0, [0, 1])
        away = [jnp.where(zl == 0, total[1, g], total[0, g]) for g in range(LANES)]
        for g in range(LANES):
            lanes = pl.ds(g * 128, 128)
            mine_out[pl.ds(t * rows, rows), lanes] = jnp.where(zl == 0, total[0, g], total[1, g])
        number = LAST_SLOT[t]
        send(away, half_sent.at[number], pl.ds(2 * FULL + number, 1), last_got.at[t], last_scale.at[t], 4, half_s, fr.at[t], up(y, 1 - zl))

    def finish(t):
        if STRAIGHT[t]:
            return
        wait_bytes(tally.at[pl.ds(0, half_rows)], fr.at[t])
        for g, value in enumerate(decode(last_got.at[t, 4], last_scale.at[t, 4], rows, LANES)):
            came_out[pl.ds(t * rows, rows), pl.ds(g * 128, 128)] = value

    work = {
        "across": across, "relay": relay, "compact": compact, "share": share, "share2": share2, "multiply": multiply,
        "hop1": lambda t: hop(t, 1), "hop2": lambda t: hop(t, 2), "hop3": lambda t: hop(t, 3),
        "merge": merge, "finish": finish,
    }
    when = []
    for t in range(CHUNKS):
        plan = AHEAD | AFTER
        when += [(plan[name] + SPACING * t, i, t, name) for i, name in enumerate(work)]
    for _, _, t, name in sorted(when):
        work[name](t)

    wait_bytes(land.at[pl.ds(0, 7)], s1s.at[0])
    wait_bytes(panel.at[pl.ds(0, CHUNKS // 2), pl.ds(0, 3)], s2s.at[0])
    wait_bytes(panel.at[:, pl.ds(0, 4)], s3s.at[0])
    wait_bytes(panel.at[:, pl.ds(0, 3)], s4s.at[0])
    wait_bytes(full_sent, full_s.at[0])
    wait_bytes(half_sent, half_s.at[0])
    wait_bytes(scale_sent, scale_s.at[0])


def body(half_three, block_mask, panel_blocks):
    cols, auxw, occ = half_three.shape
    width = auxw * occ
    rows = BLK // CHUNKS
    dma = pltpu.SemaphoreType.DMA
    vmem = pltpu.VMEM
    mine, came = pl.pallas_call(
        kernel,
        out_shape=[jax.ShapeDtypeStruct((BLK, cols), jnp.float32)] * 2,
        in_specs=[
            pl.BlockSpec(memory_space=pltpu.HBM),
            pl.BlockSpec(memory_space=pltpu.HBM),
            pl.BlockSpec(memory_space=pltpu.HBM),
        ],
        out_specs=[pl.BlockSpec(memory_space=pltpu.VMEM)] * 2,
        scratch_shapes=[
            vmem((4, BLK, auxw, occ), jnp.bfloat16),
            vmem((8, BLK, 128), jnp.bfloat16),
            vmem((4, BLK, width), jnp.bfloat16),
            vmem((BLK, width), jnp.bfloat16),
            vmem((CHUNKS, K8, NPB * rows, 128), jnp.bfloat16),
            vmem((CHUNKS, LANES, NPB, rows, 128), jnp.float32),
            vmem((FULL, 8 * rows, 128), jnp.int16),
            vmem((FULL, 8 * rows, 128), jnp.int16),
            vmem((HALF, 4 * rows, 128), jnp.int16),
            vmem((2 * CHUNKS, 4 * rows, 128), jnp.int16),
            vmem((CHUNKS, 5, 4 * rows, 128), jnp.int16),
            vmem((2 * FULL + HALF, 1, 128), jnp.float32),
            vmem((FULL, 2, 1, 128), jnp.float32),
            vmem((2 * CHUNKS, 1, 1, 128), jnp.float32),
            vmem((CHUNKS, 5, 1, 1, 128), jnp.float32),
            vmem((5 * (2 * rows + 1), 1, 128), jnp.float32),
            dma((1,)), dma((2,)), dma((1,)), dma((CHUNKS,)), dma((CHUNKS,)),
            dma((1,)), dma((CHUNKS,)), dma((CHUNKS,)), dma((1,)), dma((CHUNKS,)),
            dma((1,)), dma((1,)), dma((1,)), dma((CHUNKS, HOPS)), dma((CHUNKS,)), dma((6,)),
            vmem((1, 2, 4), jnp.int32), pltpu.SMEM((NPB,), jnp.int32),
            *[vmem((32, rows, 128), jnp.bfloat16) for _ in range(CHUNKS)],
        ],
        compiler_params=pltpu.CompilerParams(
            collective_id=0, has_side_effects=True, vmem_limit_bytes=24 << 20
        ),
        cost_estimate=pl.CostEstimate(flops=2 * 2048 * cols * width, bytes_accessed=2 << 20, transcendentals=0),
    )(pltpu.with_memory_space_constraint(half_three, pltpu.HBM), pltpu.with_memory_space_constraint(block_mask.transpose(1, 2, 0), pltpu.HBM), pltpu.with_memory_space_constraint(panel_blocks, pltpu.HBM))
    return mine + came


def solution(mesh):
    placed = (P("basis", "aux", None), P("basis", "aux", None), P())
    return jax.shard_map(
        body, mesh=mesh, in_specs=placed, out_specs=P("aux", "basis"), check_vma=False
    )
```

```python
import functools

import jax
import jax.numpy as jnp
from jax import lax
from jax.experimental import pallas as pl
from jax.experimental.pallas import tpu as pltpu
from jax.sharding import PartitionSpec as P

MESH = pl.DeviceIdType.MESH
NZH, NX, NCORE, NZL, NY = 4, 4, 2, 2, 8
NPB = 16
BLK = 128
K8 = 8
CHUNKS = 8
LANES = 4
TOP = 32767.0
ORDER = [
    (0, 0), (0, 1), (0, 4), (1, 0), (0, 2), (1, 1), (1, 4), (0, 5), (2, 0), (1, 2), (0, 3),
    (2, 1), (0, 7), (2, 4), (3, 0), (1, 5), (2, 2), (0, 6), (1, 3), (3, 1), (3, 4), (2, 5),
    (1, 7), (4, 0), (1, 6), (3, 2), (5, 0), (4, 1), (2, 3), (4, 4), (5, 1), (3, 5), (2, 7),
    (5, 4), (6, 0), (4, 2), (2, 6), (5, 2), (6, 1), (3, 3), (4, 5), (6, 4), (7, 0), (3, 7),
    (5, 5), (3, 6), (6, 2), (4, 3), (7, 1), (7, 4), (5, 3), (4, 7), (6, 5), (4, 6), (8, 0),
    (5, 7), (5, 6), (8, 1), (6, 3), (7, 5), (6, 7), (6, 6), (7, 2), (9, 1), (7, 3), (8, 5),
    (7, 7), (7, 6), (8, 4), (10, 1), (8, 2), (8, 3), (9, 0), (9, 5), (8, 7), (8, 6), (9, 4),
    (9, 2), (9, 3), (9, 7), (10, 7), (10, 4), (9, 6), (10, 0), (10, 2), (10, 5), (10, 3), (10, 6),
]
RELAY_Z = [True] * CHUNKS
RELAY_X = [True] * CHUNKS
STRAIGHT = [t >= CHUNKS - 2 for t in range(CHUNKS)]
HOPS = 4
FULL = sum(4 if straight else 6 for straight in STRAIGHT)
FULL_SLOT = [sum(4 if s else 6 for s in STRAIGHT[:t]) for t in range(CHUNKS)]
LAST_SLOT = [2 * CHUNKS + sum(5 if s else 1 for s in STRAIGHT[:t]) for t in range(CHUNKS)]
HALF = 2 * CHUNKS + sum(5 if s else 1 for s in STRAIGHT)


def rank(zh, x, c):
    return (zh * NX + x) * NCORE + c


def wait_bytes(view, sem):
    pltpu.make_async_copy(view, view, sem).wait()


def encode(values, rows, message, scale):
    for n in range(0, len(values), LANES):
        block = values[n : n + LANES]
        most = functools.reduce(jnp.maximum, [jnp.abs(value) for value in block])
        most = jnp.maximum(jnp.max(most, axis=0, keepdims=True), 1e-33)
        scale[n // LANES] = most
        factor = TOP / most
        for i, value in enumerate(block):
            coded = jnp.round(value * factor).astype(jnp.int32).astype(jnp.int16)
            message[pl.ds((n + i) * rows, rows), :] = coded


def decode(message, scale, rows, count):
    factors = [scale[n] * (1.0 / TOP) for n in range(count // LANES)]
    return [
        message[pl.ds(i * rows, rows), :].astype(jnp.int32).astype(jnp.float32) * factors[i // LANES]
        for i in range(count)
    ]


def kernel(
    half, mask_in, blocks_in, mine_out, came_out, raw, land, kept, slot, panel, part,
    full_sent, full_got, half_sent, half_got, last_got,
    scale_sent, full_scale, half_scale, last_scale, tally,
    s1s, s1r, s2s, s2n, s2f, s3s, s3n, s3f, s4s, s4r, full_s, half_s, scale_s, rsr, fr, load, mask, blocks, *stage,
):
    rows = BLK // CHUNKS
    b, a = lax.axis_index("basis"), lax.axis_index("aux")
    zh, x, c = b // (NX * NCORE), (b // NCORE) % NX, b % NCORE
    zl, y = a // NY, a % NY
    def at(zh_, x_, c_):
        return (rank(zh_, x_, c_), a)

    def up(y_, zl_=zl):
        return (b, zl_ * NY + y_)

    row_mates = [(dx, dc) for dx in (2, 1, 3, 0) for dc in range(NCORE) if dx or dc]
    barrier = pltpu.get_barrier_semaphore()
    mates = [at((zh + d) % NZH, x, c) for d in ((1, 3) if all(RELAY_Z) else (2, 1, 3))]
    mates += [up((y + d) % NY, 1 - zl) for d in ((1, NY - 1) if any(STRAIGHT) else ())]
    mates += [up((y + d) % NY) for d in (1, NY - 1)] + [up(y, 1 - zl)]
    mates += [at(zh, (x + dx) % NX, (c + dc) % NCORE) for dx, dc in row_mates]
    for mate in mates:
        pl.semaphore_signal(barrier, inc=1, device_id=mate, device_id_type=MESH)

    small = [pltpu.make_async_copy(mask_in, mask, load.at[4]), pltpu.make_async_copy(blocks_in, blocks, load.at[5])]
    for copy in small:
        copy.start()
    for w in range(4):
        pltpu.make_async_copy(half.at[pl.ds(w * BLK, BLK)], raw.at[w], load.at[w]).start()
    for copy in small:
        copy.wait()
    keeps = [[mask[0, o : o + 1, w : w + 1].astype(jnp.float32) for o in range(2)] for w in range(4)]
    within = jnp.int32(0)
    for j in range(NPB):
        within = within + jnp.where((blocks[j] >> 2) == b, blocks[j] & 3, 0)
    for w in range(4):
        wait_bytes(raw.at[w], load.at[w])

    def masked(block, keep):
        flat = block.reshape(BLK, 1024)
        both = jnp.concatenate([jnp.broadcast_to(k, (1, 128)) for k in keep] * 4, axis=1)
        return flat * both.astype(jnp.bfloat16)

    slot_keep = [sum(jnp.where(within == w, keeps[w][o], 0.0) for w in range(4)) for o in range(2)]
    slot[...] = masked(raw[within], slot_keep)
    pl.semaphore_wait(barrier, len(mates))

    def remote(src, dst, send, recv, mate):
        pltpu.make_async_remote_copy(
            src_ref=src, dst_ref=dst, send_sem=send, recv_sem=recv, device_id=mate, device_id_type=MESH
        ).start()

    eighth = 4 * c + x
    spans = [pl.ds(0, rows), pl.ds(rows, BLK - rows)]
    for i, span in enumerate(spans):
        for dx, dc in row_mates:
            x_, c_ = (x + dx) % NX, (c + dc) % NCORE
            lanes = pl.ds(pl.multiple_of((4 * c_ + x_) * 128, 128), 128)
            remote(slot.at[span, lanes], land.at[x * 2 + c, span], s1s.at[0], s1r.at[i], at(zh, x_, c_))
    land[x * 2 + c] = slot[:, pl.ds(pl.multiple_of(eighth * 128, 128), 128)]
    for w in range(4):
        kept[w] = masked(raw[w], keeps[w])

    def across(t):
        if t < 2:
            wait_bytes(land.at[pl.ds(0, 7), spans[t]], s1r.at[t])
        stage[t][pl.ds(zh * 8, 8)] = land[:, pl.ds(t * rows, rows)]
        mine = stage[t].at[pl.ds(zh * 8, 8)]
        remote(mine, mine, s2s.at[0], s2n.at[t], at((zh + 1) % NZH, x, c))
        remote(mine, mine, s2s.at[0], s2n.at[t], at((zh + 3) % NZH, x, c))
        if not RELAY_Z[t]:
            remote(mine, mine, s2s.at[0], s2f.at[t], at((zh + 2) % NZH, x, c))

    def relay(t):
        wait_bytes(stage[t].at[pl.ds(0, 16)], s2n.at[t])
        for i, d in enumerate((3, 1)):
            origin = ((zh + d) % NZH) * 8
            if RELAY_Z[t]:
                view = stage[t].at[pl.ds(origin + 4 * i, 4)]
                remote(view, view, s2s.at[0], s2f.at[t], at((zh + 4 - d) % NZH, x, c))

    def compact(t):
        wait_bytes(stage[t].at[pl.ds(((zh + 2) % NZH) * 8, 8)], s2f.at[t])
        for j in range(NPB):
            panel[t, eighth, pl.ds(j * rows, rows), :] = stage[t][blocks[j] >> 2]
        mine = panel.at[t, eighth]
        remote(mine, mine, s3s.at[0], s3n.at[t], at(zh, (x + 1) % NX, c))
        remote(mine, mine, s3s.at[0], s3n.at[t], at(zh, (x + 3) % NX, c))
        if not RELAY_X[t]:
            remote(mine, mine, s3s.at[0], s3f.at[t], at(zh, (x + 2) % NX, c))
        remote(mine, mine, s3s.at[0], s4r.at[t], at(zh, x, 1 - c))

    def share(t):
        wait_bytes(panel.at[t, pl.ds(0, 2)], s3n.at[t])
        for i, d in enumerate((3, 1)):
            origin = 4 * c + (x + d) % NX
            came = panel.at[t, origin]
            if RELAY_X[t]:
                view = panel.at[t, origin, pl.ds(8 * rows * i, 8 * rows)]
                remote(view, view, s3s.at[0], s3f.at[t], at(zh, (x + 4 - d) % NX, c))
            remote(came, came, s4s.at[0], s4r.at[t], at(zh, x, 1 - c))

    def share2(t):
        came = panel.at[t, 4 * c + (x + 2) % NX]
        wait_bytes(came, s3f.at[t])
        remote(came, came, s4s.at[0], s4r.at[t], at(zh, x, 1 - c))

    def multiply(t):
        wait_bytes(panel.at[t, pl.ds(0, 4)], s4r.at[t])
        lhs = jnp.concatenate([panel[t, k] for k in range(K8)], axis=1)
        value = lax.dot_general(
            lhs, kept[...].reshape(4 * BLK, 1024), (((1,), (1,)), ((), ())), preferred_element_type=jnp.float32
        )
        for g in range(LANES):
            part[t, g] = value[:, g * 128 : (g + 1) * 128].reshape(NPB, rows, 128)
        hop(t, 0)
        if STRAIGHT[t]:
            send_last(t, 2, 1 - zl, [part[t, g, y + NY * (1 - zl)] for g in range(LANES)])

    full_rows, half_rows = 4 * rows + 2, 2 * rows + 1

    def slots(t, step):
        return 2 * t if step == 0 else FULL_SLOT[t] + 2 * (step - 1)

    def gathered(t, step, way, halves):
        dest = (y + (HOPS - step) * (1 - 2 * way) + NY) % NY
        total = {(h, g): part[t, g, dest + NY * h] for h in halves for g in range(LANES)}
        if step == 0:
            return total
        for w in (0, 1) if step == HOPS else (way,):
            at_slot = slots(t, step - 1) + w
            got, scale = (half_got, half_scale) if step == 1 else (full_got, full_scale)
            came_halves = [w] if step == 1 else [0, 1]
            came = decode(got.at[at_slot], scale.at[at_slot], rows, LANES * len(came_halves))
            for i, h in enumerate(came_halves):
                for g in range(LANES):
                    total[h, g] = total[h, g] + came[i * LANES + g]
        return total

    def arrive(t, step):
        wait_bytes(tally.at[pl.ds(0, 2 * (half_rows if step == 0 else full_rows))], rsr.at[t, step])

    def hop(t, step):
        if step:
            arrive(t, step - 1)
        for way in range(2):
            total = gathered(t, step, way, [way] if step == 0 else [0, 1])
            values = [v for _, v in sorted(total.items())]
            mate_y = (y + (1 if way == 0 else NY - 1)) % NY
            if step == HOPS - 1 and STRAIGHT[t]:
                for h in range(2):
                    send_last(t, way, h, values[LANES * h : LANES * h + LANES], mate_y)
                continue
            at_slot = slots(t, step) + way
            if step == 0:
                send(values, half_sent.at[at_slot], pl.ds(2 * FULL + at_slot, 1), half_got, half_scale, at_slot, half_s, rsr.at[t, step], up(mate_y))
            else:
                send(values, full_sent.at[at_slot], pl.ds(2 * at_slot, 2), full_got, full_scale, at_slot, full_s, rsr.at[t, step], up(mate_y))

    def send(values, message, number, got, got_scale, where, sem, recv, mate):
        encode(values, rows, message, scale_sent.at[number])
        remote(message, got.at[where], sem.at[0], recv, mate)
        remote(scale_sent.at[number], got_scale.at[where], scale_s.at[0], recv, mate)

    def send_last(t, way, h, values, mate_y=None):
        to = y if mate_y is None else mate_y
        at_slot = 4 if way == 2 else way + 2 * ((h + zl) % 2)
        number = LAST_SLOT[t] + (4 if way == 2 else way + 2 * h)
        send(values, half_sent.at[number], pl.ds(2 * FULL + number, 1), last_got.at[t], last_scale.at[t], at_slot, half_s, fr.at[t], up(to, h))

    def merge(t):
        if STRAIGHT[t]:
            wait_bytes(tally.at[pl.ds(0, 5 * half_rows)], fr.at[t])
            for g in range(LANES):
                mine_out[pl.ds(t * rows, rows), pl.ds(g * 128, 128)] = part[t, g, y + NY * zl]
            came = [decode(last_got.at[t, i], last_scale.at[t, i], rows, LANES) for i in range(5)]
            for g in range(LANES):
                came_out[pl.ds(t * rows, rows), pl.ds(g * 128, 128)] = sum(part_[g] for part_ in came)
            return
        arrive(t, HOPS - 1)
        total = gathered(t, HOPS, 0, [0, 1])
        away = [jnp.where(zl == 0, total[1, g], total[0, g]) for g in range(LANES)]
        for g in range(LANES):
            lanes = pl.ds(g * 128, 128)
            mine_out[pl.ds(t * rows, rows), lanes] = jnp.where(zl == 0, total[0, g], total[1, g])
        number = LAST_SLOT[t]
        send(away, half_sent.at[number], pl.ds(2 * FULL + number, 1), last_got.at[t], last_scale.at[t], 4, half_s, fr.at[t], up(y, 1 - zl))

    def finish(t):
        if STRAIGHT[t]:
            return
        wait_bytes(tally.at[pl.ds(0, half_rows)], fr.at[t])
        for g, value in enumerate(decode(last_got.at[t, 4], last_scale.at[t, 4], rows, LANES)):
            came_out[pl.ds(t * rows, rows), pl.ds(g * 128, 128)] = value

    work = {
        "across": across, "relay": relay, "compact": compact, "share": share, "share2": share2, "multiply": multiply,
        "hop1": lambda t: hop(t, 1), "hop2": lambda t: hop(t, 2), "hop3": lambda t: hop(t, 3),
        "merge": merge, "finish": finish,
    }
    names = list(work)
    for stage_number, t in ORDER:
        work[names[stage_number]](t)

    wait_bytes(land.at[pl.ds(0, 7)], s1s.at[0])
    wait_bytes(panel.at[pl.ds(0, CHUNKS // 2), pl.ds(0, 3)], s2s.at[0])
    wait_bytes(panel.at[:, pl.ds(0, 4)], s3s.at[0])
    wait_bytes(panel.at[:, pl.ds(0, 3)], s4s.at[0])
    wait_bytes(full_sent, full_s.at[0])
    wait_bytes(half_sent, half_s.at[0])
    wait_bytes(scale_sent, scale_s.at[0])


def body(half_three, block_mask, panel_blocks):
    cols, auxw, occ = half_three.shape
    width = auxw * occ
    rows = BLK // CHUNKS
    dma = pltpu.SemaphoreType.DMA
    vmem = pltpu.VMEM
    mine, came = pl.pallas_call(
        kernel,
        out_shape=[jax.ShapeDtypeStruct((BLK, cols), jnp.float32)] * 2,
        in_specs=[
            pl.BlockSpec(memory_space=pltpu.HBM),
            pl.BlockSpec(memory_space=pltpu.HBM),
            pl.BlockSpec(memory_space=pltpu.HBM),
        ],
        out_specs=[pl.BlockSpec(memory_space=pltpu.VMEM)] * 2,
        scratch_shapes=[
            vmem((4, BLK, auxw, occ), jnp.bfloat16),
            vmem((8, BLK, 128), jnp.bfloat16),
            vmem((4, BLK, width), jnp.bfloat16),
            vmem((BLK, width), jnp.bfloat16),
            vmem((CHUNKS, K8, NPB * rows, 128), jnp.bfloat16),
            vmem((CHUNKS, LANES, NPB, rows, 128), jnp.float32),
            vmem((FULL, 8 * rows, 128), jnp.int16),
            vmem((FULL, 8 * rows, 128), jnp.int16),
            vmem((HALF, 4 * rows, 128), jnp.int16),
            vmem((2 * CHUNKS, 4 * rows, 128), jnp.int16),
            vmem((CHUNKS, 5, 4 * rows, 128), jnp.int16),
            vmem((2 * FULL + HALF, 1, 128), jnp.float32),
            vmem((FULL, 2, 1, 128), jnp.float32),
            vmem((2 * CHUNKS, 1, 1, 128), jnp.float32),
            vmem((CHUNKS, 5, 1, 1, 128), jnp.float32),
            vmem((5 * (2 * rows + 1), 1, 128), jnp.float32),
            dma((1,)), dma((2,)), dma((1,)), dma((CHUNKS,)), dma((CHUNKS,)),
            dma((1,)), dma((CHUNKS,)), dma((CHUNKS,)), dma((1,)), dma((CHUNKS,)),
            dma((1,)), dma((1,)), dma((1,)), dma((CHUNKS, HOPS)), dma((CHUNKS,)), dma((6,)),
            vmem((1, 2, 4), jnp.int32), pltpu.SMEM((NPB,), jnp.int32),
            *[vmem((32, rows, 128), jnp.bfloat16) for _ in range(CHUNKS)],
        ],
        compiler_params=pltpu.CompilerParams(
            collective_id=0, has_side_effects=True, vmem_limit_bytes=24 << 20
        ),
        cost_estimate=pl.CostEstimate(flops=2 * 2048 * cols * width, bytes_accessed=2 << 20, transcendentals=0),
    )(pltpu.with_memory_space_constraint(half_three, pltpu.HBM), pltpu.with_memory_space_constraint(block_mask.transpose(1, 2, 0), pltpu.HBM), pltpu.with_memory_space_constraint(panel_blocks, pltpu.HBM))
    return mine + came


def solution(mesh):
    placed = (P("basis", "aux", None), P("basis", "aux", None), P())
    return jax.shard_map(
        body, mesh=mesh, in_specs=placed, out_specs=P("aux", "basis"), check_vma=False
    )
```

```python
import functools

import jax
import jax.numpy as jnp
from jax import lax
from jax.experimental import pallas as pl
from jax.experimental.pallas import tpu as pltpu
from jax.sharding import PartitionSpec as P

MESH = pl.DeviceIdType.MESH
NZH, NX, NCORE, NZL, NY = 4, 4, 2, 2, 8
NPB = 16
BLK = 128
K8 = 8
CHUNKS = 8
LANES = 4
TOP = 32767.0
ORDER = [
    (0, 0), (0, 1), (0, 4), (1, 0), (0, 2), (1, 1), (1, 4), (0, 5), (2, 0), (1, 2), (0, 3),
    (2, 1), (0, 7), (2, 4), (3, 0), (1, 5), (2, 2), (0, 6), (1, 3), (3, 1), (3, 4), (2, 5),
    (1, 7), (4, 0), (1, 6), (3, 2), (5, 0), (4, 1), (2, 3), (4, 4), (5, 1), (3, 5), (2, 7),
    (5, 4), (6, 0), (4, 2), (2, 6), (5, 2), (6, 1), (3, 3), (4, 5), (6, 4), (7, 0), (3, 7),
    (5, 5), (3, 6), (6, 2), (4, 3), (7, 1), (7, 4), (5, 3), (4, 7), (6, 5), (4, 6), (8, 0),
    (5, 7), (5, 6), (8, 1), (6, 3), (7, 5), (6, 7), (6, 6), (7, 2), (9, 1), (7, 3), (8, 5),
    (7, 7), (7, 6), (8, 4), (10, 1), (8, 2), (8, 3), (9, 0), (9, 5), (8, 7), (8, 6), (9, 4),
    (9, 2), (9, 3), (9, 7), (10, 7), (10, 4), (9, 6), (10, 0), (10, 2), (10, 5), (10, 3), (10, 6),
]
RELAY_Z = [True] * CHUNKS
RELAY_X = [True] * CHUNKS
STRAIGHT = [t >= CHUNKS - 2 for t in range(CHUNKS)]
HOPS = 4
FULL = sum(4 if straight else 6 for straight in STRAIGHT)
FULL_SLOT = [sum(4 if s else 6 for s in STRAIGHT[:t]) for t in range(CHUNKS)]
LAST_SLOT = [2 * CHUNKS + sum(5 if s else 1 for s in STRAIGHT[:t]) for t in range(CHUNKS)]
HALF = 2 * CHUNKS + sum(5 if s else 1 for s in STRAIGHT)


def rank(zh, x, c):
    return (zh * NX + x) * NCORE + c


def wait_bytes(view, sem):
    pltpu.make_async_copy(view, view, sem).wait()


def encode(values, rows, message, scale):
    for n in range(0, len(values), LANES):
        block = values[n : n + LANES]
        most = functools.reduce(jnp.maximum, [jnp.abs(value) for value in block])
        most = jnp.maximum(jnp.max(most, axis=0, keepdims=True), 1e-33)
        scale[n // LANES] = most
        factor = TOP / most
        for i, value in enumerate(block):
            coded = jnp.round(value * factor).astype(jnp.int32).astype(jnp.int16)
            message[pl.ds((n + i) * rows, rows), :] = coded


def decode(message, scale, rows, count):
    factors = [scale[n] * (1.0 / TOP) for n in range(count // LANES)]
    return [
        message[pl.ds(i * rows, rows), :].astype(jnp.int32).astype(jnp.float32) * factors[i // LANES]
        for i in range(count)
    ]


def kernel(
    half, mask_in, blocks_in, out, raw, land, kept, slot, panel, part,
    full_sent, full_got, half_sent, half_got, last_got,
    scale_sent, full_scale, half_scale, last_scale, tally,
    s1s, s1r, s2s, s2n, s2f, s3s, s3n, s3f, s4s, s4r, full_s, half_s, scale_s, rsr, fr, load, mask, blocks, *stage,
):
    rows = BLK // CHUNKS
    b, a = lax.axis_index("basis"), lax.axis_index("aux")
    zh, x, c = b // (NX * NCORE), (b // NCORE) % NX, b % NCORE
    zl, y = a // NY, a % NY
    def at(zh_, x_, c_):
        return (rank(zh_, x_, c_), a)

    def up(y_, zl_=zl):
        return (b, zl_ * NY + y_)

    row_mates = [(dx, dc) for dx in (2, 1, 3, 0) for dc in range(NCORE) if dx or dc]
    barrier = pltpu.get_barrier_semaphore()
    mates = [at((zh + d) % NZH, x, c) for d in ((1, 3) if all(RELAY_Z) else (2, 1, 3))]
    mates += [up((y + d) % NY, 1 - zl) for d in ((1, NY - 1) if any(STRAIGHT) else ())]
    mates += [up((y + d) % NY) for d in (1, NY - 1)] + [up(y, 1 - zl)]
    mates += [at(zh, (x + dx) % NX, (c + dc) % NCORE) for dx, dc in row_mates]
    for mate in mates:
        pl.semaphore_signal(barrier, inc=1, device_id=mate, device_id_type=MESH)

    small = [pltpu.make_async_copy(mask_in, mask, load.at[4]), pltpu.make_async_copy(blocks_in, blocks, load.at[5])]
    for copy in small:
        copy.start()
    for w in range(4):
        pltpu.make_async_copy(half.at[pl.ds(w * BLK, BLK)], raw.at[w], load.at[w]).start()
    for copy in small:
        copy.wait()
    keeps = [[mask[0, o : o + 1, w : w + 1].astype(jnp.float32) for o in range(2)] for w in range(4)]
    within = jnp.int32(0)
    for j in range(NPB):
        within = within + jnp.where((blocks[j] >> 2) == b, blocks[j] & 3, 0)
    for w in range(4):
        wait_bytes(raw.at[w], load.at[w])

    def masked(block, keep):
        flat = block.reshape(BLK, 1024)
        both = jnp.concatenate([jnp.broadcast_to(k, (1, 128)) for k in keep] * 4, axis=1)
        return flat * both.astype(jnp.bfloat16)

    slot_keep = [sum(jnp.where(within == w, keeps[w][o], 0.0) for w in range(4)) for o in range(2)]
    slot[...] = masked(raw[within], slot_keep)
    pl.semaphore_wait(barrier, len(mates))

    def remote(src, dst, send, recv, mate):
        pltpu.make_async_remote_copy(
            src_ref=src, dst_ref=dst, send_sem=send, recv_sem=recv, device_id=mate, device_id_type=MESH
        ).start()

    eighth = 4 * c + x
    spans = [pl.ds(0, rows), pl.ds(rows, BLK - rows)]
    for i, span in enumerate(spans):
        for dx, dc in row_mates:
            x_, c_ = (x + dx) % NX, (c + dc) % NCORE
            lanes = pl.ds(pl.multiple_of((4 * c_ + x_) * 128, 128), 128)
            remote(slot.at[span, lanes], land.at[x * 2 + c, span], s1s.at[0], s1r.at[i], at(zh, x_, c_))
    land[x * 2 + c] = slot[:, pl.ds(pl.multiple_of(eighth * 128, 128), 128)]
    for w in range(4):
        kept[w] = masked(raw[w], keeps[w])

    def across(t):
        if t < 2:
            wait_bytes(land.at[pl.ds(0, 7), spans[t]], s1r.at[t])
        stage[t][pl.ds(zh * 8, 8)] = land[:, pl.ds(t * rows, rows)]
        mine = stage[t].at[pl.ds(zh * 8, 8)]
        remote(mine, mine, s2s.at[0], s2n.at[t], at((zh + 1) % NZH, x, c))
        remote(mine, mine, s2s.at[0], s2n.at[t], at((zh + 3) % NZH, x, c))
        if not RELAY_Z[t]:
            remote(mine, mine, s2s.at[0], s2f.at[t], at((zh + 2) % NZH, x, c))

    def relay(t):
        wait_bytes(stage[t].at[pl.ds(0, 16)], s2n.at[t])
        for i, d in enumerate((3, 1)):
            origin = ((zh + d) % NZH) * 8
            if RELAY_Z[t]:
                view = stage[t].at[pl.ds(origin + 4 * i, 4)]
                remote(view, view, s2s.at[0], s2f.at[t], at((zh + 4 - d) % NZH, x, c))

    def compact(t):
        wait_bytes(stage[t].at[pl.ds(((zh + 2) % NZH) * 8, 8)], s2f.at[t])
        for j in range(NPB):
            panel[t, eighth, pl.ds(j * rows, rows), :] = stage[t][blocks[j] >> 2]
        mine = panel.at[t, eighth]
        remote(mine, mine, s3s.at[0], s3n.at[t], at(zh, (x + 1) % NX, c))
        remote(mine, mine, s3s.at[0], s3n.at[t], at(zh, (x + 3) % NX, c))
        if not RELAY_X[t]:
            remote(mine, mine, s3s.at[0], s3f.at[t], at(zh, (x + 2) % NX, c))
        remote(mine, mine, s3s.at[0], s4r.at[t], at(zh, x, 1 - c))

    def share(t):
        wait_bytes(panel.at[t, pl.ds(0, 2)], s3n.at[t])
        for i, d in enumerate((3, 1)):
            origin = 4 * c + (x + d) % NX
            came = panel.at[t, origin]
            if RELAY_X[t]:
                view = panel.at[t, origin, pl.ds(8 * rows * i, 8 * rows)]
                remote(view, view, s3s.at[0], s3f.at[t], at(zh, (x + 4 - d) % NX, c))
            remote(came, came, s4s.at[0], s4r.at[t], at(zh, x, 1 - c))

    def share2(t):
        came = panel.at[t, 4 * c + (x + 2) % NX]
        wait_bytes(came, s3f.at[t])
        remote(came, came, s4s.at[0], s4r.at[t], at(zh, x, 1 - c))

    def multiply(t):
        wait_bytes(panel.at[t, pl.ds(0, 4)], s4r.at[t])
        lhs = jnp.concatenate([panel[t, k] for k in range(K8)], axis=1)
        value = lax.dot_general(
            lhs, kept[...].reshape(4 * BLK, 1024), (((1,), (1,)), ((), ())), preferred_element_type=jnp.float32
        )
        for g in range(LANES):
            part[t, g] = value[:, g * 128 : (g + 1) * 128].reshape(NPB, rows, 128)
        hop(t, 0)
        if STRAIGHT[t]:
            send_last(t, 2, 1 - zl, [part[t, g, y + NY * (1 - zl)] for g in range(LANES)])

    full_rows, half_rows = 4 * rows + 2, 2 * rows + 1

    def slots(t, step):
        return 2 * t if step == 0 else FULL_SLOT[t] + 2 * (step - 1)

    def gathered(t, step, way, halves):
        dest = (y + (HOPS - step) * (1 - 2 * way) + NY) % NY
        total = {(h, g): part[t, g, dest + NY * h] for h in halves for g in range(LANES)}
        if step == 0:
            return total
        for w in (0, 1) if step == HOPS else (way,):
            at_slot = slots(t, step - 1) + w
            got, scale = (half_got, half_scale) if step == 1 else (full_got, full_scale)
            came_halves = [w] if step == 1 else [0, 1]
            came = decode(got.at[at_slot], scale.at[at_slot], rows, LANES * len(came_halves))
            for i, h in enumerate(came_halves):
                for g in range(LANES):
                    total[h, g] = total[h, g] + came[i * LANES + g]
        return total

    def arrive(t, step):
        wait_bytes(tally.at[pl.ds(0, 2 * (half_rows if step == 0 else full_rows))], rsr.at[t, step])

    def hop(t, step):
        if step:
            arrive(t, step - 1)
        for way in range(2):
            total = gathered(t, step, way, [way] if step == 0 else [0, 1])
            values = [v for _, v in sorted(total.items())]
            mate_y = (y + (1 if way == 0 else NY - 1)) % NY
            if step == HOPS - 1 and STRAIGHT[t]:
                for h in range(2):
                    send_last(t, way, h, values[LANES * h : LANES * h + LANES], mate_y)
                continue
            at_slot = slots(t, step) + way
            if step == 0:
                send(values, half_sent.at[at_slot], pl.ds(2 * FULL + at_slot, 1), half_got, half_scale, at_slot, half_s, rsr.at[t, step], up(mate_y))
            else:
                send(values, full_sent.at[at_slot], pl.ds(2 * at_slot, 2), full_got, full_scale, at_slot, full_s, rsr.at[t, step], up(mate_y))

    def send(values, message, number, got, got_scale, where, sem, recv, mate):
        encode(values, rows, message, scale_sent.at[number])
        remote(message, got.at[where], sem.at[0], recv, mate)
        remote(scale_sent.at[number], got_scale.at[where], scale_s.at[0], recv, mate)

    def send_last(t, way, h, values, mate_y=None):
        to = y if mate_y is None else mate_y
        at_slot = 4 if way == 2 else way + 2 * ((h + zl) % 2)
        number = LAST_SLOT[t] + (4 if way == 2 else way + 2 * h)
        send(values, half_sent.at[number], pl.ds(2 * FULL + number, 1), last_got.at[t], last_scale.at[t], at_slot, half_s, fr.at[t], up(to, h))

    def merge(t):
        if STRAIGHT[t]:
            wait_bytes(tally.at[pl.ds(0, 5 * half_rows)], fr.at[t])
            came = [decode(last_got.at[t, i], last_scale.at[t, i], rows, LANES) for i in range(5)]
            for g in range(LANES):
                out[pl.ds(t * rows, rows), pl.ds(g * 128, 128)] = part[t, g, y + NY * zl] + sum(part_[g] for part_ in came)
            return
        arrive(t, HOPS - 1)
        total = gathered(t, HOPS, 0, [0, 1])
        away = [jnp.where(zl == 0, total[1, g], total[0, g]) for g in range(LANES)]
        for g in range(LANES):
            lanes = pl.ds(g * 128, 128)
            out[pl.ds(t * rows, rows), lanes] = jnp.where(zl == 0, total[0, g], total[1, g])
        number = LAST_SLOT[t]
        send(away, half_sent.at[number], pl.ds(2 * FULL + number, 1), last_got.at[t], last_scale.at[t], 4, half_s, fr.at[t], up(y, 1 - zl))

    def finish(t):
        if STRAIGHT[t]:
            return
        wait_bytes(tally.at[pl.ds(0, half_rows)], fr.at[t])
        for g, value in enumerate(decode(last_got.at[t, 4], last_scale.at[t, 4], rows, LANES)):
            out[pl.ds(t * rows, rows), pl.ds(g * 128, 128)] += value

    work = {
        "across": across, "relay": relay, "compact": compact, "share": share, "share2": share2, "multiply": multiply,
        "hop1": lambda t: hop(t, 1), "hop2": lambda t: hop(t, 2), "hop3": lambda t: hop(t, 3),
        "merge": merge, "finish": finish,
    }
    names = list(work)
    for stage_number, t in ORDER:
        work[names[stage_number]](t)

    wait_bytes(land.at[pl.ds(0, 7)], s1s.at[0])
    wait_bytes(panel.at[pl.ds(0, CHUNKS // 2), pl.ds(0, 3)], s2s.at[0])
    wait_bytes(panel.at[:, pl.ds(0, 4)], s3s.at[0])
    wait_bytes(panel.at[:, pl.ds(0, 3)], s4s.at[0])
    wait_bytes(full_sent, full_s.at[0])
    wait_bytes(half_sent, half_s.at[0])
    wait_bytes(scale_sent, scale_s.at[0])


def body(half_three, block_mask, panel_blocks):
    cols, auxw, occ = half_three.shape
    width = auxw * occ
    rows = BLK // CHUNKS
    dma = pltpu.SemaphoreType.DMA
    vmem = pltpu.VMEM
    return pl.pallas_call(
        kernel,
        out_shape=jax.ShapeDtypeStruct((BLK, cols), jnp.float32),
        in_specs=[
            pl.BlockSpec(memory_space=pltpu.HBM),
            pl.BlockSpec(memory_space=pltpu.HBM),
            pl.BlockSpec(memory_space=pltpu.HBM),
        ],
        out_specs=pl.BlockSpec(memory_space=pltpu.VMEM),
        scratch_shapes=[
            vmem((4, BLK, auxw, occ), jnp.bfloat16),
            vmem((8, BLK, 128), jnp.bfloat16),
            vmem((4, BLK, width), jnp.bfloat16),
            vmem((BLK, width), jnp.bfloat16),
            vmem((CHUNKS, K8, NPB * rows, 128), jnp.bfloat16),
            vmem((CHUNKS, LANES, NPB, rows, 128), jnp.float32),
            vmem((FULL, 8 * rows, 128), jnp.int16),
            vmem((FULL, 8 * rows, 128), jnp.int16),
            vmem((HALF, 4 * rows, 128), jnp.int16),
            vmem((2 * CHUNKS, 4 * rows, 128), jnp.int16),
            vmem((CHUNKS, 5, 4 * rows, 128), jnp.int16),
            vmem((2 * FULL + HALF, 1, 128), jnp.float32),
            vmem((FULL, 2, 1, 128), jnp.float32),
            vmem((2 * CHUNKS, 1, 1, 128), jnp.float32),
            vmem((CHUNKS, 5, 1, 1, 128), jnp.float32),
            vmem((5 * (2 * rows + 1), 1, 128), jnp.float32),
            dma((1,)), dma((2,)), dma((1,)), dma((CHUNKS,)), dma((CHUNKS,)),
            dma((1,)), dma((CHUNKS,)), dma((CHUNKS,)), dma((1,)), dma((CHUNKS,)),
            dma((1,)), dma((1,)), dma((1,)), dma((CHUNKS, HOPS)), dma((CHUNKS,)), dma((6,)),
            vmem((1, 2, 4), jnp.int32), pltpu.SMEM((NPB,), jnp.int32),
            *[vmem((32, rows, 128), jnp.bfloat16) for _ in range(CHUNKS)],
        ],
        compiler_params=pltpu.CompilerParams(
            collective_id=0, has_side_effects=True, vmem_limit_bytes=24 << 20
        ),
        cost_estimate=pl.CostEstimate(flops=2 * 2048 * cols * width, bytes_accessed=2 << 20, transcendentals=0),
    )(pltpu.with_memory_space_constraint(half_three, pltpu.HBM), pltpu.with_memory_space_constraint(block_mask.transpose(1, 2, 0), pltpu.HBM), pltpu.with_memory_space_constraint(panel_blocks, pltpu.HBM))


def solution(mesh):
    placed = (P("basis", "aux", None), P("basis", "aux", None), P())
    return jax.shard_map(
        body, mesh=mesh, in_specs=placed, out_specs=P("aux", "basis"), check_vma=False
    )
```
